128 devices in a mesh: wide: 32 (over y, z, core), narrow: 4 (over x).
Axes of the slice: x: 4, y: 4, z: 4, core: 2. Of those that a mesh axis runs over, the one named last changes fastest.
Arguments:
- tensor: float32 [32, 128, 256, 672], P('narrow', 'wide'), may hold values from -6 to 6
- mode2_factor: float32 [128, 96], replicated, may hold values from -0.5 to 0.5
- mode3_factor: float32 [256, 96], replicated, may hold values from -0.375 to 0.375
- mode4_factor: float32 [32, 16], replicated, may hold values from -1 to 1
- start_basis: float32 [672, 96], replicated, may hold values from -6 to 6
Outputs:
- scaled_basis: float32 [672, 96], replicated
The draws below stay inside these ranges and needn't reach their ends.
All inputs are finite; a program needn't handle non-finite values.
Results may differ from the reference program's by a relative error of at most 0.0003.
Values sent between devices are 32-bit elements; how exact they have to be, the bound alone decides.
No kernel may reach another device: no remote copies, remote signals or barrier semaphores. Data moves between devices by JAX's collectives and lax.ppermute only.
A program may use at most 192 MiB of HBM per device.

```python
import math
import jax
import jax.numpy as jnp
from jax import lax

I1 = 672
R1 = 96
R2 = 96
R3 = 96
R4 = 16
SPEC = 32
I3 = 256
ITERS = 8
I2 = 128


def level_of(rng, dims, shards, smallest, high):
    def one(position, parts):
        heights = jax.random.uniform(jax.random.fold_in(jax.random.fold_in(rng, 6), position), (parts,), jnp.float32, smallest / len(shards), high / len(shards))
        return jnp.repeat(jnp.exp(heights), dims[position] // parts).reshape((-1,) + (1,) * (len(dims) - position - 1))

    level = one(*shards[0])
    for cut in shards[1:]:
        level = level * one(*cut)
    return level


def bell_draw(rng, shape, width, most, split=(), kind=jnp.bfloat16):
    values = jax.random.normal(rng, shape, jnp.float32) * width
    if len(split) > 0:
        values = level_of(rng, shape, split, -0.22, 0.18) * values
    return jnp.clip(values, min=-most, max=most).astype(kind)


def setup_inputs(seed: int = 0) -> dict:
    arg_keys = jax.random.split(jax.random.key(seed), 6)
    tensor = bell_draw(arg_keys[0], (SPEC, I2, I3, I1), 1.0, 6.0, ((0, 4), (1, 32)), jnp.float32)
    mode2_factor = bell_draw(arg_keys[1], (I2, R2), I2 ** -0.5, 0.5, (), jnp.float32)
    mode3_factor = bell_draw(arg_keys[2], (I3, R3), I3 ** -0.5, 0.375, (), jnp.float32)
    mode4_factor = bell_draw(arg_keys[3], (SPEC, R4), SPEC ** -0.5, 1.0, (), jnp.float32)
    start_basis = bell_draw(arg_keys[4], (I1, R1), 1.0, 6.0, (), jnp.float32)
    return {"tensor": tensor, "mode2_factor": mode2_factor, "mode3_factor": mode3_factor, "mode4_factor": mode4_factor, "start_basis": start_basis}


def orthonormal(vectors):
    highest = lax.Precision.HIGHEST
    inner = lax.dot_general(vectors, vectors, (((0,), (0,)), ((), ())), precision=highest)
    lower_factor = jnp.linalg.cholesky(inner)
    return lax.linalg.triangular_solve(lower_factor, vectors, left_side=False, lower=True, transpose_a=True)

def reference(tensor, mode2_factor, mode3_factor, mode4_factor, start_basis):
    highest = lax.Precision.HIGHEST

    def species_step(carry, inputs):
        slab, weights = inputs
        by_mode3 = jnp.einsum('bka,kr->bra', slab, mode3_factor, precision=highest)
        by_mode2 = jnp.einsum('bra,bp->rpa', by_mode3, mode2_factor, precision=highest)
        return (carry + weights[None, :, None, None] * by_mode2[:, None, :, :], None)
    initial = jnp.zeros((R3, R4, R2, I1), jnp.float32)
    core_block, unused = lax.scan(species_step, initial, (tensor, mode4_factor))
    columns_flat = core_block.reshape(R3 * R4 * R2, I1)
    gram_matrix = lax.dot_general(columns_flat, columns_flat, (((0,), (0,)), ((), ())), precision=highest) / (R2 * R3 * R4)
    basis_now = start_basis
    for sweep in range(ITERS):
        basis_now = orthonormal(jnp.dot(gram_matrix, basis_now, precision=highest))
    return basis_now * math.sqrt(I1)
```

```python
import functools
import math

import jax
import jax.numpy as jnp
from jax import lax
from jax.experimental import pallas as pl
from jax.experimental.pallas import tpu as pltpu
from jax.sharding import PartitionSpec as P

I1 = 672
I2 = 128
I3 = 256
R1 = 96
R2 = 96
R3 = 96
R4 = 16
ITERS = 8
NARROW = 4
WIDE = 32
LANES = 128
FULL = I1 // LANES
TAIL = I1 - FULL * LANES
BODY = FULL * LANES
LOCAL2 = I2 // WIDE
RANKS = R3 // NARROW
PAIRS = RANKS * R4 // WIDE
ORDER = (0, 3, 1, 2)
LAST = LOCAL2 - 1
VMEM = pl.BlockSpec(memory_space=pltpu.VMEM)


def split(x):
    high = x.astype(jnp.bfloat16)
    return high, (x - high.astype(jnp.float32)).astype(jnp.bfloat16)


def product(a, b, contract):
    return lax.dot_general(
        a, b, ((contract), ((), ())), preferred_element_type=jnp.float32
    )


def exact(a, b, contract):
    return lax.dot_general(
        a, b, ((contract), ((), ())),
        preferred_element_type=jnp.float32, precision=lax.Precision.HIGHEST,
    )


def left_product(weights, values):
    rows = weights.shape[0]
    w_high, w_low = split(weights)
    v_high, v_low = split(values)
    both = product(jnp.concatenate([w_high, w_low], axis=0), v_high, ((1,), (0,)))
    return both[:rows] + both[rows:] + product(w_high, v_low, ((1,), (0,)))


def mode3_kernel(tails, factor_ref, slab_ref, *refs):
    if tails:
        tail_ref, outs = refs[0], refs[1:]
        left_over = [tail_ref[0, b, :, :TAIL] for b in range(LOCAL2)]
        slab = jnp.concatenate([slab_ref[0, 0]] + left_over, axis=1)
    else:
        outs = refs
        slab = slab_ref[0, 0]
    done = left_product(factor_ref[...], slab)
    for j, out in enumerate(outs):
        out[0] = done[j * RANKS:(j + 1) * RANKS]


def mode3(tensor, factor_rows, cell):
    species = tensor.shape[0]
    tails = cell == LAST
    width = BODY + (LANES if tails else 0)
    in_specs = [
        pl.BlockSpec((R3, I3), lambda s: (0, 0)),
        pl.BlockSpec((1, 1, I3, BODY), lambda s: (s, cell, 0, 0)),
    ]
    args = [factor_rows, tensor]
    if tails:
        in_specs.append(pl.BlockSpec((1, LOCAL2, I3, LANES), lambda s: (s, 0, 0, FULL)))
        args.append(tensor)
    shape = jax.ShapeDtypeStruct((species, RANKS, width), jnp.float32)
    return pl.pallas_call(
        functools.partial(mode3_kernel, tails),
        grid=(species,),
        in_specs=in_specs,
        out_specs=[pl.BlockSpec((1, RANKS, width), lambda s: (s, 0, 0))] * NARROW,
        out_shape=[shape] * NARROW,
        compiler_params=pltpu.CompilerParams(vmem_limit_bytes=32 << 20),
        cost_estimate=pl.CostEstimate(
            flops=6 * species * R3 * I3 * width,
            bytes_accessed=4 * species * width * (I3 + R3), transcendentals=0),
        name="mode3",
    )(*args)


def species_kernel(tiles, weights_ref, *refs):
    parts, out = refs[:NARROW], refs[NARROW]
    step = pl.program_id(0)
    rows = [p[...].reshape(-1, tiles * LANES) for p in parts]
    done = left_product(weights_ref[...], jnp.concatenate(rows, axis=0))

    def put(dest, first, q, start, count):
        for t in range(tiles):
            out[dest, t * PAIRS + first:t * PAIRS + first + count, :] = done[
                q * 8 + start:q * 8 + start + count, t * LANES:(t + 1) * LANES]

    @pl.when(step == 0)
    def _():
        spare = out.shape[1] - tiles * PAIRS
        if spare:
            out[:, tiles * PAIRS:, :] = jnp.zeros((WIDE, spare, LANES), jnp.float32)
        for q in range(R4):
            put(2 * q, 0, q, 0, 8)

    @pl.when(step == 1)
    def _():
        for q in range(R4):
            put(2 * q, 8, q, 0, 4)
            put(2 * q + 1, 0, q, 4, 4)

    @pl.when(step == 2)
    def _():
        for q in range(R4):
            put(2 * q + 1, 4, q, 0, 8)


def species_sum(parts, weights):
    species, ranks, width = parts[0].shape
    tiles = width // LANES
    rows = -(-tiles * PAIRS // 8) * 8
    return pl.pallas_call(
        functools.partial(species_kernel, tiles),
        grid=(ranks // 8,),
        in_specs=[pl.BlockSpec(weights.shape, lambda i: (0, 0))]
        + [pl.BlockSpec((species, 8, width), lambda i: (0, i, 0))] * NARROW,
        out_specs=pl.BlockSpec((WIDE, rows, LANES), lambda i: (0, 0, 0)),
        out_shape=jax.ShapeDtypeStruct((WIDE, rows, LANES), jnp.float32),
        compiler_params=pltpu.CompilerParams(vmem_limit_bytes=32 << 20),
        cost_estimate=pl.CostEstimate(
            flops=6 * 128 * 256 * 3 * width, bytes_accessed=4 * width * 24 * 48, transcendentals=0),
        name="species",
    )(weights, *parts)


def gram_kernel(factor_ref, *refs):
    parts = refs[:LOCAL2]
    out, high_ref, low_ref, gram_ref = refs[LOCAL2:]
    f_high, f_low = split(factor_ref[...])
    doubled = jnp.concatenate([f_high, f_high], axis=1)
    stride = [p.shape[0] // WIDE for p in parts]
    for i in range(PAIRS):
        tail = parts[LAST][pl.ds(FULL * PAIRS + i, WIDE, stride=stride[LAST]), :]
        cells = []
        for b in range(LOCAL2):
            row = [parts[b][pl.ds(t * PAIRS + i, WIDE, stride=stride[b]), :] for t in range(FULL)]
            row.append(tail[:, b * TAIL:(b + 1) * TAIL])
            cells.append(jnp.concatenate(row, axis=1))
        values = jnp.concatenate(cells, axis=0)
        v_high, v_low = split(values)
        core = product(doubled, jnp.concatenate([v_high, v_low], axis=0), ((1,), (0,)))
        core = core + product(f_low, v_high, ((1,), (0,)))
        c_high, c_low = split(core)
        high_ref[i * R2:(i + 1) * R2, :] = c_high
        low_ref[i * R2:(i + 1) * R2, :] = c_low
    edges = (0, 256, 512, I1)
    for bi in range(3):
        left = slice(edges[bi], edges[bi + 1])
        for bj in range(bi, 3):
            right = slice(edges[bj], edges[bj + 1])
            rows0 = ((0,), (0,))
            gram_ref[left, right] = (
                product(high_ref[:, left], high_ref[:, right], rows0)
                + product(high_ref[:, left], low_ref[:, right], rows0)
                + product(low_ref[:, left], high_ref[:, right], rows0)
            )
    n = 0
    for i in range(FULL):
        for j in range(i, FULL):
            out[n * LANES:(n + 1) * LANES, :] = gram_ref[
                i * LANES:(i + 1) * LANES, j * LANES:(j + 1) * LANES]
            n += 1
    edge = gram_ref[:BODY, BODY:]
    out[n * LANES:(n + 1) * LANES, :] = jnp.concatenate(
        [edge[k * LANES:(k + 1) * LANES] for k in range(4)], axis=1)
    out[64:128, :64] = jnp.concatenate([edge[512:576], edge[576:640]], axis=1)
    out[FULL * LANES + 64:FULL * LANES + 96, :TAIL] = gram_ref[BODY:, BODY:]


def gram_part(parts, factor_rows):
    rows = PAIRS * R2
    return pl.pallas_call(
        gram_kernel,
        in_specs=[VMEM] * (1 + LOCAL2),
        out_specs=VMEM,
        out_shape=jax.ShapeDtypeStruct((16 * LANES, LANES), jnp.float32),
        scratch_shapes=[
            pltpu.VMEM((rows, I1), jnp.bfloat16),
            pltpu.VMEM((rows, I1), jnp.bfloat16),
            pltpu.VMEM((I1, I1), jnp.float32),
        ],
        compiler_params=pltpu.CompilerParams(vmem_limit_bytes=40 << 20),
        name="gram",
    )(factor_rows, *parts)


def add_kernel(x_ref, o_ref):
    devices = x_ref.shape[0]
    total = jnp.sum(x_ref[...], axis=0) * (1.0 / (R2 * R3 * R4))
    o_ref[...] = jnp.broadcast_to(total[None], (devices,) + total.shape)


def add_parts(x):
    return pl.pallas_call(
        add_kernel, in_specs=[VMEM], out_specs=VMEM,
        out_shape=jax.ShapeDtypeStruct(x.shape, jnp.float32),
        compiler_params=pltpu.CompilerParams(vmem_limit_bytes=32 << 20),
        name="add",
    )(x)


def inverse_factor(a):
    n = a.shape[0]
    blocks = n // 8
    rows = [a[8 * i:8 * i + 8, :] for i in range(blocks)]
    lane = lax.broadcasted_iota(jnp.int32, (8, n), 1)
    sub = lax.broadcasted_iota(jnp.int32, (8, n), 0)
    spread = lambda x: jnp.broadcast_to(x, (8, n))
    pivots = []
    for k in range(blocks):
        cols = [[spread(rows[i][:, 8 * k + j:8 * k + j + 1]) for j in range(8)]
                for i in range(k, blocks)]
        inside = (lane >= 8 * k) & (lane < 8 * k + 8)
        rows[k] = jnp.where(inside, jnp.where(lane - 8 * k == sub, 1.0, 0.0), rows[k])
        for i in range(k + 1, blocks):
            rows[i] = jnp.where(inside, 0.0, rows[i])
        pivot = jnp.zeros((8, n), jnp.float32)
        for j in range(8):
            here = cols[0][j]
            pivot = jnp.where(sub == j, here, pivot)
            inverse = 1.0 / spread(here[j:j + 1, :])
            pivot_row = spread(rows[k][j:j + 1, :])
            pivot_cols = {m: spread(cols[0][m][j:j + 1, :]) for m in range(j + 1, 8)}
            for i in range(k, blocks):
                f = cols[i - k][j] * inverse
                if i == k:
                    f = jnp.where(sub > j, f, 0.0)
                rows[i] = rows[i] - f * pivot_row
                for m in range(j + 1, 8):
                    cols[i - k][m] = cols[i - k][m] - f * pivot_cols[m]
        pivots.append(pivot)
    return jnp.concatenate(
        [jnp.where(lane <= sub + 8 * k, rows[k] * lax.rsqrt(pivots[k]), 0.0)
         for k in range(blocks)], axis=0)


def sweep_kernel(packed_ref, start_ref, out_ref, gram_ref, basis_ref):
    n = 0
    row = lax.broadcasted_iota(jnp.int32, (LANES, LANES), 0)
    col = lax.broadcasted_iota(jnp.int32, (LANES, LANES), 1)
    for i in range(FULL):
        for j in range(i, FULL):
            tile = packed_ref[n * LANES:(n + 1) * LANES, :]
            here = slice(i * LANES, (i + 1) * LANES)
            there = slice(j * LANES, (j + 1) * LANES)
            if i == j:
                above = jnp.where(row < col, tile, 0.0)
                gram_ref[here, here] = jnp.where(row <= col, tile, 0.0) + above.T
            else:
                gram_ref[here, there] = tile
                gram_ref[there, here] = tile.T
            n += 1
    last = packed_ref[n * LANES:(n + 1) * LANES, :]
    for k in range(4):
        gram_ref[k * LANES:(k + 1) * LANES, BODY:] = last[:, k * TAIL:(k + 1) * TAIL]
    gram_ref[512:576, BODY:] = packed_ref[64:128, :TAIL]
    gram_ref[576:640, BODY:] = packed_ref[64:128, TAIL:2 * TAIL]
    gram_ref[BODY:, BODY:] = packed_ref[FULL * LANES + 64:FULL * LANES + 96, :TAIL]
    gram_ref[BODY:, :BODY] = gram_ref[:BODY, BODY:].T
    basis_ref[...] = start_ref[...].T

    def sweep(_, carry):
        image = exact(basis_ref[...], gram_ref[...], ((1,), (0,)))
        inner = exact(image, image, ((1,), (1,)))
        basis_ref[...] = exact(inverse_factor(inner), image, ((1,), (0,)))
        return carry

    lax.fori_loop(0, ITERS, sweep, 0)
    out_ref[...] = (basis_ref[...] * math.sqrt(I1)).T


def sweeps(packed, start_basis):
    return pl.pallas_call(
        sweep_kernel, in_specs=[VMEM, VMEM], out_specs=VMEM,
        out_shape=jax.ShapeDtypeStruct((I1, R1), jnp.float32),
        scratch_shapes=[
            pltpu.VMEM((I1, I1), jnp.float32), pltpu.VMEM((R1, I1), jnp.float32)],
        compiler_params=pltpu.CompilerParams(vmem_limit_bytes=32 << 20),
        name="sweeps",
    )(packed, start_basis)


def factors(mode2_factor, mode3_factor, mode4_factor, me):
    turned = jnp.transpose(mode3_factor)
    turned = lax.dynamic_slice_in_dim(
        jnp.concatenate([turned, turned], axis=0), me * RANKS, R3, 0)
    species = mode4_factor.shape[0]
    local = species // NARROW
    blocks = mode4_factor.reshape(NARROW, local, R4)[::-1].reshape(species, R4)
    blocks = lax.dynamic_slice_in_dim(
        jnp.concatenate([blocks, blocks], axis=0), (NARROW - 1 - me) * local, species, 0)
    weights = jnp.transpose(blocks)[:, None, :, None] * jnp.eye(8, dtype=jnp.float32)[None, :, None, :]
    weights = weights.reshape(R4 * 8, species * 8)
    cells = jnp.transpose(mode2_factor.reshape(WIDE, LOCAL2, R2), (2, 1, 0)).reshape(R2, I2)
    return turned, weights, cells


def body(tensor, mode2_factor, mode3_factor, mode4_factor, start_basis):
    me = lax.axis_index("narrow")
    turned, weights, cells = factors(mode2_factor, mode3_factor, mode4_factor, me)
    parts = [None] * LOCAL2
    before = None
    for cell in ORDER:
        blocks = mode3(tensor, turned, cell)
        if before is not None:
            blocks, before = lax.optimization_barrier((blocks, before))
        got = [blocks[0]]
        for j in range(1, NARROW):
            ring = [(i, (i + j) % NARROW) for i in range(NARROW)]
            got.append(lax.ppermute(blocks[j], "narrow", ring))
        before = got[1:]
        sums = species_sum(got, weights)
        sums = lax.all_to_all(sums, "wide", 0, 0, tiled=True)
        parts[cell] = sums.reshape(-1, LANES)
    packed = gram_part(parts, cells)
    everyone = ("wide", "narrow")
    packed = packed.reshape(WIDE * NARROW, -1, LANES)
    packed = add_parts(lax.all_to_all(packed, everyone, 0, 0, tiled=True))
    packed = lax.all_to_all(packed, everyone, 0, 0, tiled=True)
    return sweeps(packed.reshape(-1, LANES), start_basis)


def solution(mesh):
    in_specs = (P("narrow", "wide", None, None), P(), P(), P(), P())
    return jax.shard_map(body, mesh=mesh, in_specs=in_specs, out_specs=P(), check_vma=False)
```

```python
import functools
import math

import jax
import jax.numpy as jnp
from jax import lax
from jax.experimental import pallas as pl
from jax.experimental.pallas import tpu as pltpu
from jax.sharding import PartitionSpec as P

I1 = 672
I2 = 128
I3 = 256
R1 = 96
R2 = 96
R3 = 96
R4 = 16
ITERS = 8
NARROW = 4
WIDE = 32
LANES = 128
FULL = I1 // LANES
TAIL = I1 - FULL * LANES
BODY = FULL * LANES
LOCAL2 = I2 // WIDE
RANKS = R3 // NARROW
PAIRS = RANKS * R4 // WIDE
CHUNKS = ((0, 1), (2, 3), (4,))
FIRST = FULL - 1
SPECIES_COST = 10 ** 11
VMEM = pl.BlockSpec(memory_space=pltpu.VMEM)


def whole(x):
    return pl.BlockSpec(x.shape, lambda i: (0,) * len(x.shape))


def split(x):
    high = x.astype(jnp.bfloat16)
    return high, (x - high.astype(jnp.float32)).astype(jnp.bfloat16)


def product(a, b, contract):
    return lax.dot_general(
        a, b, ((contract), ((), ())), preferred_element_type=jnp.float32
    )


def exact(a, b, contract):
    return lax.dot_general(
        a, b, ((contract), ((), ())),
        preferred_element_type=jnp.float32, precision=lax.Precision.HIGHEST,
    )


def left_product(weights, values):
    rows = weights.shape[0]
    w_high, w_low = split(weights)
    v_high, v_low = split(values)
    both = product(jnp.concatenate([w_high, w_low], axis=0), v_high, ((1,), (0,)))
    return both[:rows] + both[rows:] + product(w_high, v_low, ((1,), (0,)))


def mode3_kernel(factor_ref, *refs):
    outs, slabs = refs[-NARROW:], refs[:-NARROW]
    f_high, f_low = split(factor_ref[...])
    lanes = ((1,), (1,))
    for s in range(outs[0].shape[0]):
        rows = [slab[s].reshape(-1, I3) for slab in slabs]
        rows = rows[0] if len(rows) == 1 else jnp.concatenate(rows, axis=0)
        r_high, r_low = split(rows)
        both = product(jnp.concatenate([f_high, f_low], axis=0), r_high, lanes)
        done = both[:R3] + both[R3:] + product(f_high, r_low, lanes)
        for j, out in enumerate(outs):
            out[s] = done[j * RANKS:(j + 1) * RANKS]


def mode3(field, factor_rows, chunk):
    species = field.shape[0]
    count = len(chunk)
    index = chunk[0] // count
    width = LOCAL2 * LANES * count
    some = species // 2 // count
    in_specs = [
        pl.BlockSpec((R3, I3), lambda s: (0, 0)),
        pl.BlockSpec((some, LOCAL2, LANES * count, I3), lambda s: (s, 0, index, 0)),
    ]
    args = [factor_rows, field]
    if chunk == CHUNKS[-1]:
        width += LANES
        in_specs.append(pl.BlockSpec((some, LOCAL2, TAIL, I3), lambda s: (s, 0, BODY // TAIL, 0)))
        args.append(field)
    shape = jax.ShapeDtypeStruct((species, RANKS, width), jnp.float32)
    return pl.pallas_call(
        mode3_kernel,
        grid=(species // some,),
        in_specs=in_specs,
        out_specs=[pl.BlockSpec((some, RANKS, width), lambda s: (s, 0, 0))] * NARROW,
        out_shape=[shape] * NARROW,
        compiler_params=pltpu.CompilerParams(vmem_limit_bytes=48 << 20),
        cost_estimate=pl.CostEstimate(
            flops=6 * species * R3 * I3 * width,
            bytes_accessed=4 * species * width * (I3 + R3), transcendentals=0),
        name="mode3",
    )(*args)


def species_kernel(tiles, weights_ref, *refs):
    parts, out = refs[:NARROW], refs[NARROW]
    step = pl.program_id(0)
    rows = [p[...].reshape(-1, tiles * LANES) for p in parts]
    done = left_product(weights_ref[...], jnp.concatenate(rows, axis=0))

    def put(dest, first, q, start, count):
        for t in range(tiles):
            out[dest, t * PAIRS + first:t * PAIRS + first + count, :] = done[
                q * 8 + start:q * 8 + start + count, t * LANES:(t + 1) * LANES]

    @pl.when(step == 0)
    def _():
        spare = out.shape[1] - tiles * PAIRS
        if spare:
            out[:, tiles * PAIRS:, :] = jnp.zeros((WIDE, spare, LANES), jnp.float32)
        for q in range(R4):
            put(2 * q, 0, q, 0, 8)

    @pl.when(step == 1)
    def _():
        for q in range(R4):
            put(2 * q, 8, q, 0, 4)
            put(2 * q + 1, 0, q, 4, 4)

    @pl.when(step == 2)
    def _():
        for q in range(R4):
            put(2 * q + 1, 4, q, 0, 8)


def species_sum(parts, weights):
    species, ranks, width = parts[0].shape
    tiles = width // LANES
    rows = -(-tiles * PAIRS // 8) * 8
    return pl.pallas_call(
        functools.partial(species_kernel, tiles),
        grid=(ranks // 8,),
        in_specs=[pl.BlockSpec(weights.shape, lambda i: (0, 0))]
        + [pl.BlockSpec((species, 8, width), lambda i: (0, i, 0))] * NARROW,
        out_specs=pl.BlockSpec((WIDE, rows, LANES), lambda i: (0, 0, 0)),
        out_shape=jax.ShapeDtypeStruct((WIDE, rows, LANES), jnp.float32),
        compiler_params=pltpu.CompilerParams(vmem_limit_bytes=20 << 20),
        cost_estimate=pl.CostEstimate(
            flops=SPECIES_COST, bytes_accessed=4 * width * 24 * 48, transcendentals=0),
        name="species",
    )(weights, *parts)


def core_columns(factor, parts, last, store):
    f_high, f_low = split(factor)
    doubled = jnp.concatenate([f_high, f_high], axis=1)
    strides = [p.shape[0] // WIDE for p in parts]
    counts = [len(tiles) for tiles in (CHUNKS[-1:] if last else CHUNKS[:-1])]

    def piece(p, place):
        return parts[p][pl.ds(place, WIDE, stride=strides[p]), :]

    for i in range(PAIRS):
        cells = []
        if last:
            tail = piece(0, LOCAL2 * counts[0] * PAIRS + i)
        for b in range(LOCAL2):
            row = [piece(p, (b * n + t) * PAIRS + i) for p, n in enumerate(counts) for t in range(n)]
            if last:
                row.append(tail[:, b * TAIL:(b + 1) * TAIL])
            cells.append(jnp.concatenate(row, axis=1))
        v_high, v_low = split(jnp.concatenate(cells, axis=0))
        core = product(doubled, jnp.concatenate([v_high, v_low], axis=0), ((1,), (0,)))
        store(i, *split(core + product(f_low, v_high, ((1,), (0,)))))


def inner_product(a_high, a_low, b_high, b_low):
    rows = ((0,), (0,))
    return product(a_high, b_high, rows) + product(a_high, b_low, rows) + product(a_low, b_high, rows)


def gram_first_kernel(factor_ref, *refs):
    parts, (out, core_ref) = refs[:-2], refs[-2:]
    half = PAIRS * R2

    def store(i, high, low):
        core_ref[i * R2:(i + 1) * R2, :] = high
        core_ref[half + i * R2:half + (i + 1) * R2, :] = low

    core_columns(factor_ref[...], parts, False, store)
    place = 0
    for i in range(FIRST):
        left = slice(i * LANES, (i + 1) * LANES)
        right = slice(i * LANES, FIRST * LANES)
        block = inner_product(core_ref[:half, left], core_ref[half:, left],
                              core_ref[:half, right], core_ref[half:, right])
        for j in range(FIRST - i):
            out[place:place + LANES, :] = block[:, j * LANES:(j + 1) * LANES]
            place += LANES


def gram_last_kernel(factor_ref, part_ref, core_ref, tiles_ref, out, high_ref, low_ref):
    half = PAIRS * R2

    def store(i, high, low):
        high_ref[i * R2:(i + 1) * R2, :] = high
        low_ref[i * R2:(i + 1) * R2, :] = low

    core_columns(factor_ref[...], [part_ref], True, store)
    place = tiles_ref.shape[0]
    out[:place, :] = tiles_ref[...]
    high, low = high_ref[...], low_ref[...]
    above = inner_product(core_ref[:half, :], core_ref[half:, :], high, low)
    own = inner_product(high, low, high, low)
    out[place:place + FIRST * LANES, :] = above[:, :LANES]
    place += FIRST * LANES
    out[place:place + LANES, :] = own[:LANES, :LANES]
    edge = own[:LANES, LANES:]
    out[place + 64:place + LANES, :64] = jnp.concatenate([edge[:64], edge[64:]], axis=1)
    out[64:96, :TAIL] = own[LANES:, LANES:]
    place += LANES
    out[place:place + LANES, :] = jnp.concatenate(
        [above[i * LANES:(i + 1) * LANES, LANES:] for i in range(FIRST)], axis=1)


def gram_call(kernel, args, out_shape, scratch, flops):
    some = isinstance(out_shape, list)
    return pl.pallas_call(
        kernel, grid=(1,), in_specs=[whole(x) for x in args],
        out_specs=[whole(x) for x in out_shape] if some else whole(out_shape),
        out_shape=out_shape, scratch_shapes=scratch,
        compiler_params=pltpu.CompilerParams(vmem_limit_bytes=48 << 20),
        cost_estimate=pl.CostEstimate(flops=flops, bytes_accessed=8 << 20, transcendentals=0),
        name="gram",
    )(*args)


def gram_first(parts, factor_rows):
    rows = PAIRS * R2
    columns = FIRST * LANES
    tiles = FIRST * (FIRST + 1) // 2
    return gram_call(
        gram_first_kernel, [factor_rows, *parts],
        [jax.ShapeDtypeStruct((tiles * LANES, LANES), jnp.float32),
         jax.ShapeDtypeStruct((2 * rows, columns), jnp.bfloat16)],
        [], 4 * rows * columns * columns)


def gram_last(part, core, tiles, factor_rows):
    half = pltpu.VMEM((PAIRS * R2, LANES + TAIL), jnp.bfloat16)
    return gram_call(
        gram_last_kernel, [factor_rows, part, core, tiles],
        jax.ShapeDtypeStruct((16 * LANES, LANES), jnp.float32),
        [half, half], 6 * PAIRS * R2 * I1 * (LANES + TAIL))


def add_kernel(x_ref, o_ref):
    devices = x_ref.shape[0]
    total = jnp.sum(x_ref[...], axis=0) * (1.0 / (R2 * R3 * R4))
    o_ref[...] = jnp.broadcast_to(total[None], (devices,) + total.shape)


def add_parts(x):
    return pl.pallas_call(
        add_kernel, in_specs=[VMEM], out_specs=VMEM,
        out_shape=jax.ShapeDtypeStruct(x.shape, jnp.float32),
        compiler_params=pltpu.CompilerParams(vmem_limit_bytes=20 << 20),
        name="add",
    )(x)


def inverse_factor(a):
    n = a.shape[0]
    blocks = n // 8
    rows = [a[8 * i:8 * i + 8, :] for i in range(blocks)]
    lane = lax.broadcasted_iota(jnp.int32, (8, n), 1)
    sub = lax.broadcasted_iota(jnp.int32, (8, n), 0)
    spread = lambda x: jnp.broadcast_to(x, (8, n))
    pivots = []
    for k in range(blocks):
        cols = [[spread(rows[i][:, 8 * k + j:8 * k + j + 1]) for j in range(8)]
                for i in range(k, blocks)]
        inside = (lane >= 8 * k) & (lane < 8 * k + 8)
        rows[k] = jnp.where(inside, jnp.where(lane - 8 * k == sub, 1.0, 0.0), rows[k])
        for i in range(k + 1, blocks):
            rows[i] = jnp.where(inside, 0.0, rows[i])
        pivot = jnp.zeros((8, n), jnp.float32)
        for j in range(8):
            here = cols[0][j]
            pivot = jnp.where(sub == j, here, pivot)
            inverse = 1.0 / spread(here[j:j + 1, :])
            pivot_row = spread(rows[k][j:j + 1, :])
            pivot_cols = {m: spread(cols[0][m][j:j + 1, :]) for m in range(j + 1, 8)}
            for i in range(k, blocks):
                f = cols[i - k][j] * inverse
                if i == k:
                    f = jnp.where(sub > j, f, 0.0)
                rows[i] = rows[i] - f * pivot_row
                for m in range(j + 1, 8):
                    cols[i - k][m] = cols[i - k][m] - f * pivot_cols[m]
        pivots.append(pivot)
    return jnp.concatenate(
        [jnp.where(lane <= sub + 8 * k, rows[k] * lax.rsqrt(pivots[k]), 0.0)
         for k in range(blocks)], axis=0)


def sweep_kernel(packed_ref, start_ref, out_ref, gram_ref):
    row = lax.broadcasted_iota(jnp.int32, (LANES, LANES), 0)
    col = lax.broadcasted_iota(jnp.int32, (LANES, LANES), 1)
    place = 0
    pairs = [(i, j) for i in range(FIRST) for j in range(i, FIRST)]
    pairs += [(i, FIRST) for i in range(FIRST + 1)]
    for i, j in pairs:
        tile = packed_ref[place:place + LANES, :]
        here = slice(i * LANES, (i + 1) * LANES)
        there = slice(j * LANES, (j + 1) * LANES)
        if i == j:
            above = jnp.where(row < col, tile, 0.0)
            gram_ref[here, here] = jnp.where(row <= col, tile, 0.0) + above.T
        else:
            gram_ref[here, there] = tile
            gram_ref[there, here] = tile.T
        place += LANES
    last = packed_ref[place:place + LANES, :]
    for k in range(FIRST):
        gram_ref[k * LANES:(k + 1) * LANES, BODY:] = last[:, k * TAIL:(k + 1) * TAIL]
    gram_ref[512:576, BODY:] = packed_ref[place - 64:place, :TAIL]
    gram_ref[576:640, BODY:] = packed_ref[place - 64:place, TAIL:2 * TAIL]
    gram_ref[BODY:, BODY:] = packed_ref[64:96, :TAIL]
    gram_ref[BODY:, :BODY] = gram_ref[:BODY, BODY:].T
    out_ref[...] = start_ref[...]

    def sweep(_, carry):
        image = exact(out_ref[...], gram_ref[...], ((1,), (0,)))
        inner = exact(image, image, ((1,), (1,)))
        out_ref[...] = exact(inverse_factor(inner), image, ((1,), (0,)))
        return carry

    lax.fori_loop(0, ITERS, sweep, 0)
    out_ref[...] = out_ref[...] * math.sqrt(I1)


def sweeps(packed, start_rows):
    return pl.pallas_call(
        sweep_kernel, in_specs=[VMEM, VMEM], out_specs=VMEM,
        out_shape=jax.ShapeDtypeStruct((R1, I1), jnp.float32),
        scratch_shapes=[pltpu.VMEM((I1, I1), jnp.float32)],
        compiler_params=pltpu.CompilerParams(vmem_limit_bytes=20 << 20),
        name="sweeps",
    )(packed, start_rows)


def factors(mode2_factor, mode3_factor, mode4_factor, me):
    turned = jnp.transpose(mode3_factor)
    turned = lax.dynamic_slice_in_dim(
        jnp.concatenate([turned, turned], axis=0), me * RANKS, R3, 0)
    species = mode4_factor.shape[0]
    local = species // NARROW
    blocks = mode4_factor.reshape(NARROW, local, R4)[::-1].reshape(species, R4)
    blocks = lax.dynamic_slice_in_dim(
        jnp.concatenate([blocks, blocks], axis=0), (NARROW - 1 - me) * local, species, 0)
    weights = jnp.transpose(blocks)[:, None, :, None] * jnp.eye(8, dtype=jnp.float32)[None, :, None, :]
    weights = weights.reshape(R4 * 8, species * 8)
    cells = jnp.transpose(mode2_factor.reshape(WIDE, LOCAL2, R2), (2, 1, 0)).reshape(R2, I2)
    return turned, weights, cells


def body(tensor, mode2_factor, mode3_factor, mode4_factor, start_basis):
    me = lax.axis_index("narrow")
    turned, weights, cells = factors(mode2_factor, mode3_factor, mode4_factor, me)
    field = jnp.transpose(tensor, (0, 1, 3, 2))

    def send(blocks):
        got = [blocks[0]]
        for j in range(1, NARROW):
            ring = [(i, (i + j) % NARROW) for i in range(NARROW)]
            got.append(lax.ppermute(blocks[j], "narrow", ring))
        return got

    count = len(CHUNKS)
    got = send(mode3(field, turned, CHUNKS[0]))
    parts = []
    for index in range(count):
        if index + 1 < count:
            blocks = mode3(field, turned, CHUNKS[index + 1])
            coming = send(blocks)
            got, blocks = lax.optimization_barrier((got, blocks))
        sums = lax.all_to_all(species_sum(got, weights), "wide", 0, 0, tiled=True)
        got = coming
        parts.append(sums.reshape(-1, LANES))
    tiles, core = gram_first(parts[:-1], cells)
    packed = gram_last(parts[-1], core, tiles, cells)
    everyone = ("wide", "narrow")
    packed = packed.reshape(WIDE * NARROW, -1, LANES)
    packed = add_parts(lax.all_to_all(packed, everyone, 0, 0, tiled=True))
    packed = lax.all_to_all(packed, everyone, 0, 0, tiled=True)
    return jnp.transpose(sweeps(packed.reshape(-1, LANES), jnp.transpose(start_basis)))


def solution(mesh):
    in_specs = (P("narrow", "wide", None, None), P(), P(), P(), P())
    return jax.shard_map(body, mesh=mesh, in_specs=in_specs, out_specs=P(), check_vma=False)
```

```python
import functools
import math

import jax
import jax.numpy as jnp
from jax import lax
from jax.experimental import pallas as pl
from jax.experimental.pallas import tpu as pltpu
from jax.sharding import PartitionSpec as P

I1 = 672
I2 = 128
I3 = 256
R1 = 96
R2 = 96
R3 = 96
R4 = 16
ITERS = 8
NARROW = 4
WIDE = 32
WIDE_AXES = ("y", "z", "core")
CHIPS = 64
LANES = 128
FULL = I1 // LANES
TAIL = I1 - FULL * LANES
BODY = FULL * LANES
LOCAL2 = I2 // WIDE
RANKS = R3 // NARROW
PAIRS = RANKS * R4 // WIDE
CHUNKS = ((4,), (0, 1), (2, 3))
EARLY = 3 * LANES + TAIL
LATE = 2 * LANES
EARLY_TILES = ((0, 0), (0, 1), (1, 1), (0, 4), (1, 4), (4, 4))
LATE_TILES = ((0, 2), (0, 3), (1, 2), (1, 3), (4, 2), (4, 3), (2, 2), (2, 3), (3, 3))
SPECIES_COST = 10 ** 11
VMEM = pl.BlockSpec(memory_space=pltpu.VMEM)


def whole(x):
    return pl.BlockSpec(x.shape, lambda i: (0,) * len(x.shape))


def split(x):
    high = x.astype(jnp.bfloat16)
    return high, (x - high.astype(jnp.float32)).astype(jnp.bfloat16)


def product(a, b, contract):
    return lax.dot_general(
        a, b, ((contract), ((), ())), preferred_element_type=jnp.float32
    )


def exact(a, b, contract):
    return lax.dot_general(
        a, b, ((contract), ((), ())),
        preferred_element_type=jnp.float32, precision=lax.Precision.HIGHEST,
    )


def left_product(weights, values):
    rows = weights.shape[0]
    w_high, w_low = split(weights)
    v_high, v_low = split(values)
    both = product(jnp.concatenate([w_high, w_low], axis=0), v_high, ((1,), (0,)))
    return both[:rows] + both[rows:] + product(w_high, v_low, ((1,), (0,)))


def mode3_kernel(factor_ref, *refs):
    outs, slabs = refs[-NARROW:], refs[:-NARROW]
    f_high, f_low = split(factor_ref[...])
    lanes = ((1,), (1,))
    for s in range(outs[0].shape[0]):
        rows = [slab[s].reshape(-1, I3) for slab in slabs]
        rows = rows[0] if len(rows) == 1 else jnp.concatenate(rows, axis=0)
        r_high, r_low = split(rows)
        both = product(jnp.concatenate([f_high, f_low], axis=0), r_high, lanes)
        done = both[:R3] + both[R3:] + product(f_high, r_low, lanes)
        for j, out in enumerate(outs):
            out[s] = done[j * RANKS:(j + 1) * RANKS]


def mode3(field, factor_rows, chunk):
    species = field.shape[0]
    count = len(chunk)
    index = chunk[0] // count
    width = LOCAL2 * LANES * count
    some = species // 2 // count
    in_specs = [
        pl.BlockSpec((R3, I3), lambda s: (0, 0)),
        pl.BlockSpec((some, LOCAL2, LANES * count, I3), lambda s: (s, 0, index, 0)),
    ]
    args = [factor_rows, field]
    if chunk == CHUNKS[0]:
        width += LANES
        in_specs.append(pl.BlockSpec((some, LOCAL2, TAIL, I3), lambda s: (s, 0, BODY // TAIL, 0)))
        args.append(field)
    shape = jax.ShapeDtypeStruct((species, RANKS, width), jnp.float32)
    return pl.pallas_call(
        mode3_kernel,
        grid=(species // some,),
        in_specs=in_specs,
        out_specs=[pl.BlockSpec((some, RANKS, width), lambda s: (s, 0, 0))] * NARROW,
        out_shape=[shape] * NARROW,
        compiler_params=pltpu.CompilerParams(vmem_limit_bytes=48 << 20),
        cost_estimate=pl.CostEstimate(
            flops=6 * species * R3 * I3 * width,
            bytes_accessed=4 * species * width * (I3 + R3), transcendentals=0),
        name="mode3",
    )(*args)


def species_kernel(tiles, weights_ref, *refs):
    parts, out = refs[:NARROW], refs[NARROW]
    step = pl.program_id(0)
    rows = [p[...].reshape(-1, tiles * LANES) for p in parts]
    done = left_product(weights_ref[...], jnp.concatenate(rows, axis=0))

    def put(dest, first, q, start, count):
        for t in range(tiles):
            out[dest, t * PAIRS + first:t * PAIRS + first + count, :] = done[
                q * 8 + start:q * 8 + start + count, t * LANES:(t + 1) * LANES]

    @pl.when(step == 0)
    def _():
        spare = out.shape[1] - tiles * PAIRS
        if spare:
            out[:, tiles * PAIRS:, :] = jnp.zeros((WIDE, spare, LANES), jnp.float32)
        for q in range(R4):
            put(2 * q, 0, q, 0, 8)

    @pl.when(step == 1)
    def _():
        for q in range(R4):
            put(2 * q, 8, q, 0, 4)
            put(2 * q + 1, 0, q, 4, 4)

    @pl.when(step == 2)
    def _():
        for q in range(R4):
            put(2 * q + 1, 4, q, 0, 8)


def species_sum(parts, weights):
    species, ranks, width = parts[0].shape
    tiles = width // LANES
    rows = -(-tiles * PAIRS // 8) * 8
    return pl.pallas_call(
        functools.partial(species_kernel, tiles),
        grid=(ranks // 8,),
        in_specs=[pl.BlockSpec(weights.shape, lambda i: (0, 0))]
        + [pl.BlockSpec((species, 8, width), lambda i: (0, i, 0))] * NARROW,
        out_specs=pl.BlockSpec((WIDE, rows, LANES), lambda i: (0, 0, 0)),
        out_shape=jax.ShapeDtypeStruct((WIDE, rows, LANES), jnp.float32),
        compiler_params=pltpu.CompilerParams(vmem_limit_bytes=20 << 20),
        cost_estimate=pl.CostEstimate(
            flops=SPECIES_COST, bytes_accessed=4 * width * 24 * 48, transcendentals=0),
        name="species",
    )(weights, *parts)


def core_columns(factor, parts, store):
    f_high, f_low = split(factor)
    doubled = jnp.concatenate([f_high, f_high], axis=1)

    def piece(ref, place):
        return ref[pl.ds(place, WIDE, stride=ref.shape[0] // WIDE), :]

    for i in range(PAIRS):
        cells = []
        for b in range(LOCAL2):
            row = []
            for ref, count, tail in parts:
                row += [piece(ref, (b * count + t) * PAIRS + i) for t in range(count)]
                if tail:
                    last = piece(ref, LOCAL2 * count * PAIRS + i)
                    row.append(last[:, b * TAIL:(b + 1) * TAIL])
            cells.append(jnp.concatenate(row, axis=1))
        v_high, v_low = split(jnp.concatenate(cells, axis=0))
        core = product(doubled, jnp.concatenate([v_high, v_low], axis=0), ((1,), (0,)))
        store(i, *split(core + product(f_low, v_high, ((1,), (0,)))))


def inner_product(a_high, a_low, b_high, b_low):
    rows = ((0,), (0,))
    return product(a_high, b_high, rows) + product(a_high, b_low, rows) + product(a_low, b_high, rows)


def tile_of(block, i, j):
    return block[i * LANES:(i + 1) * LANES, j * LANES:(j + 1) * LANES]


def gram_first_kernel(factor_ref, edge_ref, part_ref, out, core_ref):
    half = PAIRS * R2

    def store(i, high, low):
        core_ref[i * R2:(i + 1) * R2, :] = high
        core_ref[half + i * R2:half + (i + 1) * R2, :] = low

    core_columns(factor_ref[...], ((part_ref, 2, False), (edge_ref, 1, True)), store)
    two = slice(0, LATE)
    rest = slice(LATE, EARLY)
    top = inner_product(core_ref[:half, two], core_ref[half:, two], core_ref[:half, :], core_ref[half:, :])
    own = inner_product(core_ref[:half, rest], core_ref[half:, rest],
                        core_ref[:half, rest], core_ref[half:, rest])
    tiles = [tile_of(top, 0, 0), tile_of(top, 0, 1), tile_of(top, 1, 1),
             tile_of(top, 0, 2), tile_of(top, 1, 2), own[:LANES, :LANES]]
    for n, tile in enumerate(tiles):
        out[n * LANES:(n + 1) * LANES, :] = tile
    edges = [top[:LANES, 3 * LANES:], top[LANES:, 3 * LANES:], own[:LANES, LANES:]]
    corner = own[LANES:, LANES:]
    edges.append(jnp.concatenate([corner] * (LANES // TAIL), axis=0))
    out[len(tiles) * LANES:, :] = jnp.concatenate(edges, axis=1)


def gram_last_kernel(me_ref, factor_ref, part_ref, core_ref, early_ref, keep, give, high_ref, low_ref, out):
    half = PAIRS * R2

    def store(i, high, low):
        high_ref[i * R2:(i + 1) * R2, :] = high
        low_ref[i * R2:(i + 1) * R2, :] = low

    core_columns(factor_ref[...], ((part_ref, 2, False),), store)
    place = early_ref.shape[0]
    out[:place, :] = early_ref[...]
    high, low = high_ref[...], low_ref[...]
    above = inner_product(core_ref[:half, :], core_ref[half:, :], high, low)
    own = inner_product(high, low, high, low)
    tiles = [tile_of(above, i, j) for i in range(3) for j in range(2)]
    tiles += [tile_of(own, 0, 0), tile_of(own, 0, 1), tile_of(own, 1, 1)]
    for n, tile in enumerate(tiles):
        out[place + n * LANES:place + (n + 1) * LANES, :] = tile
    left = above[3 * LANES:, :]
    for j, n in ((0, 6), (1, 8)):
        corner = place + n * LANES + 64
        out[corner:corner + TAIL, :64] = left[:, j * LANES:j * LANES + 64]
        out[corner + TAIL:corner + 2 * TAIL, :64] = left[:, j * LANES + 64:(j + 1) * LANES]
    rows = keep.shape[0]
    me = me_ref[0]
    keep[...] = out[pl.ds(pl.multiple_of(me * rows, rows), rows), :]
    give[...] = out[pl.ds(pl.multiple_of((1 - me) * rows, rows), rows), :]


def gram_call(kernel, args, out_shape, scratch, flops):
    some = isinstance(out_shape, list)
    return pl.pallas_call(
        kernel, grid=(1,),
        in_specs=[pl.BlockSpec(memory_space=pltpu.SMEM) if x.ndim == 1 else whole(x) for x in args],
        out_specs=[whole(x) for x in out_shape] if some else whole(out_shape),
        out_shape=out_shape, scratch_shapes=scratch,
        compiler_params=pltpu.CompilerParams(vmem_limit_bytes=48 << 20),
        cost_estimate=pl.CostEstimate(flops=flops, bytes_accessed=8 << 20, transcendentals=0),
        name="gram",
    )(*args)


def gram_first(parts, factor_rows):
    rows = PAIRS * R2
    return gram_call(
        gram_first_kernel, [factor_rows, *parts],
        [jax.ShapeDtypeStruct(((len(EARLY_TILES) + 1) * LANES, LANES), jnp.float32),
         jax.ShapeDtypeStruct((2 * rows, EARLY), jnp.bfloat16)],
        [], 4 * rows * EARLY * EARLY)


def gram_last(me, part, core, early, factor_rows):
    half = pltpu.VMEM((PAIRS * R2, LATE), jnp.bfloat16)
    return gram_call(
        gram_last_kernel, [me, factor_rows, part, core, early],
        [jax.ShapeDtypeStruct((8 * LANES, LANES), jnp.float32)] * 2,
        [half, half, pltpu.VMEM((16 * LANES, LANES), jnp.float32)],
        6 * PAIRS * R2 * I1 * LATE)


def add_kernel(x_ref, o_ref):
    devices = x_ref.shape[0]
    total = jnp.sum(x_ref[...], axis=0) * (1.0 / (R2 * R3 * R4))
    o_ref[...] = jnp.broadcast_to(total[None], (devices,) + total.shape)


def add_parts(x):
    return pl.pallas_call(
        add_kernel, in_specs=[VMEM], out_specs=VMEM,
        out_shape=jax.ShapeDtypeStruct(x.shape, jnp.float32),
        compiler_params=pltpu.CompilerParams(vmem_limit_bytes=20 << 20),
        name="add",
    )(x)


def three(x):
    high = x.astype(jnp.bfloat16)
    rest = x - high.astype(jnp.float32)
    middle = rest.astype(jnp.bfloat16)
    return high, middle, (rest - middle.astype(jnp.float32)).astype(jnp.bfloat16)


def times(x, parts):
    n = x.shape[0]
    x1, x2, x3 = three(x)
    rows = ((1,), (0,))
    a = product(jnp.concatenate([x1, x2, x3], axis=0), parts[0][...], rows)
    b = product(jnp.concatenate([x1, x2], axis=0), parts[1][...], rows)
    c = product(x1, parts[2][...], rows)
    return a[:n] + ((a[n:2 * n] + b[:n]) + (a[2 * n:] + b[n:] + c))


def inner_rows(x):
    high, low = split(x)
    lanes = ((1,), (1,))
    return product(high, high, lanes) + (product(high, low, lanes) + product(low, high, lanes))


def inverse_factor(a):
    n = a.shape[0]
    blocks = n // 8
    rows = [a[8 * i:8 * i + 8, :] for i in range(blocks)]
    lane = lax.broadcasted_iota(jnp.int32, (8, n), 1)
    sub = lax.broadcasted_iota(jnp.int32, (8, n), 0)
    spread = lambda x: jnp.broadcast_to(x, (8, n))
    pivots = []
    for k in range(blocks):
        cols = [[spread(rows[i][:, 8 * k + j:8 * k + j + 1]) for j in range(8)]
                for i in range(k, blocks)]
        inside = (lane >= 8 * k) & (lane < 8 * k + 8)
        rows[k] = jnp.where(inside, jnp.where(lane - 8 * k == sub, 1.0, 0.0), rows[k])
        for i in range(k + 1, blocks):
            rows[i] = jnp.where(inside, 0.0, rows[i])
        pivot = jnp.zeros((8, n), jnp.float32)
        for j in range(0, 8, 2):
            p = spread(cols[0][j][j:j + 1, :])
            q = spread(cols[0][j][j + 1:j + 2, :])
            s = spread(cols[0][j + 1][j + 1:j + 2, :])
            det = p * s - q * q
            over_p, over_det = 1.0 / p, 1.0 / det
            row0, row1 = spread(rows[k][j:j + 1, :]), spread(rows[k][j + 1:j + 2, :])
            pivot = jnp.where(sub == j, p, jnp.where(sub == j + 1, det * over_p, pivot))
            u0, u1, u2 = s * over_det, q * over_det, p * over_det
            pair = {m: (spread(cols[0][m][j:j + 1, :]), spread(cols[0][m][j + 1:j + 2, :]))
                    for m in range(j + 2, 8)}
            for i in range(k, blocks):
                c0, c1 = cols[i - k][j], cols[i - k][j + 1]
                f0, f1 = c0 * u0 - c1 * u1, c1 * u2 - c0 * u1
                if i == k:
                    f0 = jnp.where(sub > j + 1, f0, jnp.where(sub == j + 1, q * over_p, 0.0))
                    f1 = jnp.where(sub > j + 1, f1, 0.0)
                rows[i] = rows[i] - (f0 * row0 + f1 * row1)
                for m in range(j + 2, 8):
                    cols[i - k][m] = cols[i - k][m] - (f0 * pair[m][0] + f1 * pair[m][1])
        pivots.append(pivot)
    return jnp.concatenate(
        [jnp.where(lane <= sub + 8 * k, rows[k] * lax.rsqrt(pivots[k]), 0.0)
         for k in range(blocks)], axis=0)


def sweep_kernel(core_ref, mine_ref, other_ref, start_ref, out_ref, packed_ref, gram_ref, image_ref, *parts):
    half = mine_ref.shape[0]
    me = core_ref[0]
    packed_ref[pl.ds(pl.multiple_of(me * half, half), half), :] = mine_ref[...]
    packed_ref[pl.ds(pl.multiple_of((1 - me) * half, half), half), :] = other_ref[...]
    row = lax.broadcasted_iota(jnp.int32, (LANES, LANES), 0)
    col = lax.broadcasted_iota(jnp.int32, (LANES, LANES), 1)
    span = lambda i: slice(i * LANES, (i + 1) * LANES)
    edge = packed_ref[span(len(EARLY_TILES)), :]
    for n, pair in enumerate(EARLY_TILES + (None,) + LATE_TILES):
        if pair is None:
            continue
        i, j = pair
        tile = packed_ref[span(n), :]
        if i == j:
            above = jnp.where(row < col, tile, 0.0)
            gram_ref[span(i), span(i)] = jnp.where(row <= col, tile, 0.0) + above.T
        else:
            gram_ref[span(i), span(j)] = tile
            gram_ref[span(j), span(i)] = tile.T
        if i == j and i in (2, 3):
            gram_ref[BODY:, i * LANES:i * LANES + 64] = tile[64:64 + TAIL, :64]
            gram_ref[BODY:, i * LANES + 64:(i + 1) * LANES] = tile[64 + TAIL:, :64]
    for k, i in enumerate((0, 1, 4)):
        gram_ref[span(i), BODY:] = edge[:, k * TAIL:(k + 1) * TAIL]
    gram_ref[BODY:, BODY:] = edge[:TAIL, 3 * TAIL:]
    gram_ref[BODY:, :LATE] = gram_ref[:LATE, BODY:].T
    gram_ref[BODY:, span(4)] = gram_ref[span(4), BODY:].T
    gram_ref[LATE:2 * LATE, BODY:] = gram_ref[BODY:, LATE:2 * LATE].T
    for part, value in zip(parts, three(gram_ref[...])):
        part[...] = value

    image_ref[...] = times(start_ref[...], parts)

    def sweep(_, carry):
        image = image_ref[...]
        ahead = times(image, parts)
        image_ref[...] = exact(inverse_factor(inner_rows(image)), ahead, ((1,), (0,)))
        return carry

    lax.fori_loop(0, ITERS - 1, sweep, 0)
    image = image_ref[...]
    inner = exact(image, image, ((1,), (1,)))
    out_ref[...] = exact(inverse_factor(inner), image, ((1,), (0,))) * math.sqrt(I1)


def sweeps(core, mine, other, start_rows):
    return pl.pallas_call(
        sweep_kernel,
        in_specs=[pl.BlockSpec(memory_space=pltpu.SMEM), VMEM, VMEM, VMEM], out_specs=VMEM,
        out_shape=jax.ShapeDtypeStruct((R1, I1), jnp.float32),
        scratch_shapes=[
            pltpu.VMEM((16 * LANES, LANES), jnp.float32), pltpu.VMEM((I1, I1), jnp.float32),
            pltpu.VMEM((R1, I1), jnp.float32)] + [pltpu.VMEM((I1, I1), jnp.bfloat16)] * 3,
        compiler_params=pltpu.CompilerParams(vmem_limit_bytes=32 << 20),
        name="sweeps",
    )(core, mine, other, start_rows)


def factors(mode2_factor, mode3_factor, mode4_factor, me):
    turned = jnp.transpose(mode3_factor)
    turned = lax.dynamic_slice_in_dim(
        jnp.concatenate([turned, turned], axis=0), me * RANKS, R3, 0)
    species = mode4_factor.shape[0]
    local = species // NARROW
    blocks = mode4_factor.reshape(NARROW, local, R4)[::-1].reshape(species, R4)
    blocks = lax.dynamic_slice_in_dim(
        jnp.concatenate([blocks, blocks], axis=0), (NARROW - 1 - me) * local, species, 0)
    weights = jnp.transpose(blocks)[:, None, :, None] * jnp.eye(8, dtype=jnp.float32)[None, :, None, :]
    weights = weights.reshape(R4 * 8, species * 8)
    cells = jnp.transpose(mode2_factor.reshape(WIDE, LOCAL2, R2), (2, 1, 0)).reshape(R2, I2)
    return turned, weights, cells


def body(tensor, mode2_factor, mode3_factor, mode4_factor, start_basis):
    me = lax.axis_index("narrow")
    turned, weights, cells = factors(mode2_factor, mode3_factor, mode4_factor, me)
    field = jnp.transpose(tensor, (0, 1, 3, 2))

    def send(blocks):
        got = list(blocks)
        for j in (1, 3, 2):
            ring = [(i, (i + j) % NARROW) for i in range(NARROW)]
            got[j] = lax.ppermute(blocks[j], "narrow", ring)
        return got

    count = len(CHUNKS)
    got = send(mode3(field, turned, CHUNKS[0]))
    parts = []
    for index in range(count):
        if index + 1 < count:
            blocks = mode3(field, turned, CHUNKS[index + 1])
            near = [got[1], got[3]]
            near, blocks = lax.optimization_barrier((near, blocks))
            got[1], got[3] = near
            coming = send(blocks)
        sums = lax.all_to_all(species_sum(got, weights), WIDE_AXES, 0, 0, tiled=True)
        got = coming
        parts.append(sums.reshape(-1, LANES))
    early, core = gram_first(parts[:-1], cells)
    core_index = lax.axis_index("core").reshape(1)
    swap = [(0, 1), (1, 0)]
    keep, give = gram_last(core_index, parts[-1], core, early, cells)
    half = keep + lax.ppermute(give, "core", swap)
    chips = ("y", "z", "narrow")
    half = half.reshape(CHIPS, -1, LANES)
    half = add_parts(lax.all_to_all(half, chips, 0, 0, tiled=True))
    mine = lax.all_to_all(half, chips, 0, 0, tiled=True).reshape(-1, LANES)
    other = lax.ppermute(mine, "core", swap)
    return jnp.transpose(sweeps(core_index, mine, other, jnp.transpose(start_basis)))


def solution(mesh):
    fine = jax.sharding.Mesh(
        mesh.devices.reshape(4, 4, 2, NARROW), ("y", "z", "core", "narrow"))
    in_specs = (P("narrow", WIDE_AXES, None, None), P(), P(), P(), P())
    return jax.shard_map(body, mesh=fine, in_specs=in_specs, out_specs=P(), check_vma=False)
```

```python
import functools
import math

import jax
import jax.numpy as jnp
from jax import lax
from jax.experimental import pallas as pl
from jax.experimental.pallas import tpu as pltpu
from jax.sharding import PartitionSpec as P

I1 = 672
I2 = 128
I3 = 256
R1 = 96
R2 = 96
R3 = 96
R4 = 16
ITERS = 8
NARROW = 4
WIDE = 32
WIDE_AXES = ("y", "z", "core")
CHIPS = 64
LANES = 128
FULL = I1 // LANES
TAIL = I1 - FULL * LANES
BODY = FULL * LANES
LOCAL2 = I2 // WIDE
WIDE_RANKS = WIDE
NARROW_RANKS = R3 - WIDE_RANKS
RANKS = NARROW_RANKS // NARROW
PAIRS = RANKS * R4 // WIDE
SPECIES = 32
LOCAL4 = SPECIES // NARROW
SHARE = R2 // NARROW
CHUNKS = ((0, 1, 4), (2, 3))
EARLY = 3 * LANES + TAIL
LATE = 2 * LANES
EARLY_TILES = ((0, 0), (0, 1), (1, 1), (0, 4), (1, 4), (4, 4))
LATE_TILES = ((0, 2), (0, 3), (1, 2), (1, 3), (4, 2), (4, 3), (2, 2), (2, 3), (3, 3))
SPECIES_COST = 10 ** 11
VMEM = pl.BlockSpec(memory_space=pltpu.VMEM)


def whole(x):
    return pl.BlockSpec(x.shape, lambda i: (0,) * len(x.shape))


def split(x):
    high = x.astype(jnp.bfloat16)
    return high, (x - high.astype(jnp.float32)).astype(jnp.bfloat16)


def product(a, b, contract):
    return lax.dot_general(
        a, b, ((contract), ((), ())), preferred_element_type=jnp.float32
    )


def exact(a, b, contract):
    return lax.dot_general(
        a, b, ((contract), ((), ())),
        preferred_element_type=jnp.float32, precision=lax.Precision.HIGHEST,
    )


def left_product(weights, values):
    rows = weights.shape[0]
    w_high, w_low = split(weights)
    v_high, v_low = split(values)
    both = product(jnp.concatenate([w_high, w_low], axis=0), v_high, ((1,), (0,)))
    return both[:rows] + both[rows:] + product(w_high, v_low, ((1,), (0,)))


def mode3_kernel(factor_ref, *refs):
    outs, rest_out, slabs = refs[-NARROW - 1:-1], refs[-1], refs[:-NARROW - 1]
    f_high, f_low = split(factor_ref[...])
    lanes = ((1,), (1,))
    some = outs[0].shape[0]
    stride = rest_out.shape[0] // WIDE
    for s in range(some):
        rows = jnp.concatenate([slab[s].reshape(-1, I3) for slab in slabs], axis=0)
        r_high, r_low = split(rows)
        both = product(jnp.concatenate([f_high, f_low], axis=0), r_high, lanes)
        done = both[:R3] + both[R3:] + product(f_high, r_low, lanes)
        for j, out in enumerate(outs):
            out[s] = done[j * RANKS:(j + 1) * RANKS]
        place = pl.program_id(0) * some + s
        for u in range(stride // LOCAL4):
            rest_out[pl.ds(u * LOCAL4 + place, WIDE, stride=stride), :] = done[
                NARROW_RANKS:, u * LANES:(u + 1) * LANES]


def mode3(field, factor_rows, chunk):
    species = field.shape[0]
    count = len(chunk)
    width = LOCAL2 * LANES * count
    some = 2
    in_specs = [pl.BlockSpec((R3, I3), lambda s: (0, 0))]
    for tile in chunk:
        in_specs.append(pl.BlockSpec((some, LOCAL2, LANES, I3), lambda s, tile=tile: (s, 0, tile, 0)))
    if chunk == CHUNKS[0]:
        width += LANES
        in_specs.append(pl.BlockSpec((some, LOCAL2, TAIL, I3), lambda s: (s, 0, BODY // TAIL, 0)))
    args = [factor_rows] + [field] * (len(in_specs) - 1)
    shape = jax.ShapeDtypeStruct((species, RANKS, width), jnp.float32)
    rest = (WIDE * species * width // LANES, LANES)
    out = pl.pallas_call(
        mode3_kernel,
        grid=(species // some,),
        in_specs=in_specs,
        out_specs=[pl.BlockSpec((some, RANKS, width), lambda s: (s, 0, 0))] * NARROW
        + [pl.BlockSpec(rest, lambda s: (0, 0))],
        out_shape=[shape] * NARROW + [jax.ShapeDtypeStruct(rest, jnp.float32)],
        compiler_params=pltpu.CompilerParams(vmem_limit_bytes=48 << 20),
        cost_estimate=pl.CostEstimate(
            flops=6 * species * R3 * I3 * width,
            bytes_accessed=4 * species * width * (I3 + R3), transcendentals=0),
        name="mode3",
    )(*args)
    return out[:NARROW], out[NARROW].reshape(WIDE, -1, LANES)


def species_kernel(tiles, weights_ref, *refs):
    parts, out = refs[:NARROW], refs[NARROW]
    step = pl.program_id(0)
    rows = [p[...].reshape(-1, tiles * LANES) for p in parts]
    done = left_product(weights_ref[...], jnp.concatenate(rows, axis=0))
    for q in range(R4):
        for t in range(tiles):
            out[2 * q + step, t * PAIRS:(t + 1) * PAIRS, :] = done[
                q * 8:(q + 1) * 8, t * LANES:(t + 1) * LANES]


def species_sum(parts, weights, cost):
    species, ranks, width = parts[0].shape
    tiles = width // LANES
    rows = tiles * PAIRS
    return pl.pallas_call(
        functools.partial(species_kernel, tiles),
        grid=(ranks // 8,),
        in_specs=[pl.BlockSpec(weights.shape, lambda i: (0, 0))]
        + [pl.BlockSpec((species, 8, width), lambda i: (0, i, 0))] * NARROW,
        out_specs=pl.BlockSpec((WIDE, rows, LANES), lambda i: (0, 0, 0)),
        out_shape=jax.ShapeDtypeStruct((WIDE, rows, LANES), jnp.float32),
        compiler_params=pltpu.CompilerParams(vmem_limit_bytes=24 << 20),
        cost_estimate=pl.CostEstimate(
            flops=cost, bytes_accessed=4 * width * 24 * 48, transcendentals=0),
        name="species",
    )(weights, *parts)


def place_of(tile, b):
    if tile in CHUNKS[0]:
        return CHUNKS[0].index(tile) * LOCAL2 + b
    return len(CHUNKS[0]) * LOCAL2 + 1 + CHUNKS[1].index(tile) * LOCAL2 + b


def mode2_kernel(factor_ref, part_ref, *outs):
    f_high, f_low = split(factor_ref[...])
    doubled = jnp.concatenate([f_high, f_high], axis=1)
    stride = part_ref.shape[0] // WIDE
    tails = []
    for s in range(LOCAL4):
        def piece(place):
            return part_ref[pl.ds(place * LOCAL4 + s, WIDE, stride=stride), :]

        last = piece(len(CHUNKS[0]) * LOCAL2)
        cells = [
            jnp.concatenate([piece(place_of(t, b)) for t in range(FULL)]
                            + [last[:, b * TAIL:(b + 1) * TAIL]], axis=1)
            for b in range(LOCAL2)]
        v_high, v_low = split(jnp.concatenate(cells, axis=0))
        core = product(doubled, jnp.concatenate([v_high, v_low], axis=0), ((1,), (0,)))
        core = core + product(f_low, v_high, ((1,), (0,)))
        for j, out in enumerate(outs):
            rows = core[j * SHARE:(j + 1) * SHARE]
            for t in range(FULL):
                out[(s * FULL + t) * SHARE:(s * FULL + t + 1) * SHARE, :] = rows[:, t * LANES:(t + 1) * LANES]
        tails.append(core[:, BODY:])
        if s % 4 == 3:
            four = jnp.concatenate(tails[-4:], axis=1)
            start = (LOCAL4 * FULL + s // 4) * SHARE
            for j, out in enumerate(outs):
                out[start:start + SHARE, :] = four[j * SHARE:(j + 1) * SHARE]


def mode2_sum(part, factor_rows):
    rows = (LOCAL4 * FULL + LOCAL4 // 4) * SHARE
    shape = jax.ShapeDtypeStruct((rows, LANES), jnp.float32)
    args = [factor_rows, part]
    return pl.pallas_call(
        mode2_kernel, grid=(1,), in_specs=[whole(x) for x in args],
        out_specs=[whole(shape)] * NARROW, out_shape=[shape] * NARROW,
        compiler_params=pltpu.CompilerParams(vmem_limit_bytes=24 << 20),
        cost_estimate=pl.CostEstimate(
            flops=SPECIES_COST, bytes_accessed=6 << 20, transcendentals=0),
        name="mode2",
    )(*args)


def other_gram_kernel(weights_ref, *refs):
    parts, (out, high_ref, low_ref) = refs[:NARROW], refs[NARROW:]
    for block in range(SHARE // 8):
        rows = []
        for part in parts:
            for s in range(LOCAL4):
                def piece(n):
                    return part[n * SHARE + block * 8:n * SHARE + block * 8 + 8, :]

                tail = piece(LOCAL4 * FULL + s // 4)
                rows.append(jnp.concatenate(
                    [piece(s * FULL + t) for t in range(FULL)]
                    + [tail[:, s % 4 * TAIL:(s % 4 + 1) * TAIL]], axis=1))
        high, low = split(left_product(weights_ref[...], jnp.concatenate(rows, axis=0)))
        here = slice(block * R4 * 8, (block + 1) * R4 * 8)
        high_ref[here, :] = high
        low_ref[here, :] = low

    def inner(left, right):
        return inner_product(high_ref[:, left], low_ref[:, left], high_ref[:, right], low_ref[:, right])

    top = inner(slice(0, 256), slice(0, I1))
    middle = inner(slice(256, 512), slice(256, 512))
    below = inner(slice(512, I1), slice(256, I1))
    grid = {(i, j): tile_of(top, i, j) for i in range(2) for j in range(FULL)}
    grid.update({(2 + i, 2 + j): tile_of(middle, i, j) for i in range(2) for j in range(2)})
    grid.update({(4, 2 + j): tile_of(below, 0, j) for j in range(3)})
    for n, pair in enumerate(EARLY_TILES + (None,) + LATE_TILES):
        if pair is not None:
            out[n * LANES:(n + 1) * LANES, :] = grid[pair]
    put_edges(out, len(EARLY_TILES) * LANES, [top[:LANES, BODY:], top[LANES:, BODY:], below[:LANES, 256 + LANES:]],
              below[LANES:, 256 + LANES:])
    put_left(out, (len(EARLY_TILES) + 1) * LANES, below[LANES:, :256])


def other_gram(parts, weights):
    rows = SHARE * R4
    out = jax.ShapeDtypeStruct((16 * LANES, LANES), jnp.float32)
    args = [weights, *parts]
    half = pltpu.VMEM((rows, I1), jnp.bfloat16)
    return gram_call(other_gram_kernel, args, out, [half, half], 2 * SPECIES_COST)


def core_columns(factor, parts, store):
    f_high, f_low = split(factor)
    doubled = jnp.concatenate([f_high, f_high], axis=1)

    def piece(ref, place):
        return ref[pl.ds(place, WIDE, stride=ref.shape[0] // WIDE), :]

    for i in range(PAIRS):
        cells = []
        for b in range(LOCAL2):
            row = []
            for ref, count, tail in parts:
                row += [piece(ref, (t * LOCAL2 + b) * PAIRS + i) for t in range(count)]
                if tail:
                    last = piece(ref, LOCAL2 * count * PAIRS + i)
                    row.append(last[:, b * TAIL:(b + 1) * TAIL])
            cells.append(jnp.concatenate(row, axis=1))
        v_high, v_low = split(jnp.concatenate(cells, axis=0))
        core = product(doubled, jnp.concatenate([v_high, v_low], axis=0), ((1,), (0,)))
        store(i, *split(core + product(f_low, v_high, ((1,), (0,)))))


def inner_product(a_high, a_low, b_high, b_low):
    rows = ((0,), (0,))
    return product(a_high, b_high, rows) + product(a_high, b_low, rows) + product(a_low, b_high, rows)


def put_edges(out, place, edges, corner):
    edges = edges + [jnp.concatenate([corner] * (LANES // TAIL), axis=0)]
    out[place:place + LANES, :] = jnp.concatenate(edges, axis=1)


def put_left(out, place, left):
    for j, n in ((0, 6), (1, 8)):
        corner = place + n * LANES + 64
        out[corner:corner + TAIL, :64] = left[:, j * LANES:j * LANES + 64]
        out[corner + TAIL:corner + 2 * TAIL, :64] = left[:, j * LANES + 64:(j + 1) * LANES]


def tile_of(block, i, j):
    return block[i * LANES:(i + 1) * LANES, j * LANES:(j + 1) * LANES]


def gram_first_kernel(factor_ref, part_ref, out, core_ref):
    half = PAIRS * R2

    def store(i, high, low):
        core_ref[i * R2:(i + 1) * R2, :] = high
        core_ref[half + i * R2:half + (i + 1) * R2, :] = low

    core_columns(factor_ref[...], ((part_ref, 3, True),), store)
    two = slice(0, LATE)
    rest = slice(LATE, EARLY)
    top = inner_product(core_ref[:half, two], core_ref[half:, two], core_ref[:half, :], core_ref[half:, :])
    own = inner_product(core_ref[:half, rest], core_ref[half:, rest],
                        core_ref[:half, rest], core_ref[half:, rest])
    tiles = [tile_of(top, 0, 0), tile_of(top, 0, 1), tile_of(top, 1, 1),
             tile_of(top, 0, 2), tile_of(top, 1, 2), own[:LANES, :LANES]]
    for n, tile in enumerate(tiles):
        out[n * LANES:(n + 1) * LANES, :] = tile
    put_edges(out, len(tiles) * LANES,
              [top[:LANES, 3 * LANES:], top[LANES:, 3 * LANES:], own[:LANES, LANES:]], own[LANES:, LANES:])


def gram_last_kernel(me_ref, factor_ref, part_ref, core_ref, early_ref, other_ref, keep, give, high_ref, low_ref, out):
    half = PAIRS * R2

    def store(i, high, low):
        high_ref[i * R2:(i + 1) * R2, :] = high
        low_ref[i * R2:(i + 1) * R2, :] = low

    core_columns(factor_ref[...], ((part_ref, 2, False),), store)
    place = early_ref.shape[0]
    out[:place, :] = early_ref[...]
    high, low = high_ref[...], low_ref[...]
    above = inner_product(core_ref[:half, :], core_ref[half:, :], high, low)
    own = inner_product(high, low, high, low)
    tiles = [tile_of(above, i, j) for i in range(3) for j in range(2)]
    tiles += [tile_of(own, 0, 0), tile_of(own, 0, 1), tile_of(own, 1, 1)]
    for n, tile in enumerate(tiles):
        out[place + n * LANES:place + (n + 1) * LANES, :] = tile
    put_left(out, place, above[3 * LANES:, :])
    rows = keep.shape[0]
    me = me_ref[0]
    for ref, core in ((keep, me), (give, 1 - me)):
        here = pl.ds(pl.multiple_of(core * rows, rows), rows)
        ref[...] = out[here, :] + other_ref[here, :]


def gram_call(kernel, args, out_shape, scratch, flops):
    some = isinstance(out_shape, list)
    return pl.pallas_call(
        kernel, grid=(1,),
        in_specs=[pl.BlockSpec(memory_space=pltpu.SMEM) if x.ndim == 1 else whole(x) for x in args],
        out_specs=[whole(x) for x in out_shape] if some else whole(out_shape),
        out_shape=out_shape, scratch_shapes=scratch,
        compiler_params=pltpu.CompilerParams(vmem_limit_bytes=24 << 20),
        cost_estimate=pl.CostEstimate(flops=flops, bytes_accessed=8 << 20, transcendentals=0),
        name="gram",
    )(*args)


def gram_first(part, factor_rows):
    rows = PAIRS * R2
    return gram_call(
        gram_first_kernel, [factor_rows, part],
        [jax.ShapeDtypeStruct(((len(EARLY_TILES) + 1) * LANES, LANES), jnp.float32),
         jax.ShapeDtypeStruct((2 * rows, EARLY), jnp.bfloat16)],
        [], 4 * rows * EARLY * EARLY)


def gram_last(me, part, core, early, other, factor_rows):
    half = pltpu.VMEM((PAIRS * R2, LATE), jnp.bfloat16)
    return gram_call(
        gram_last_kernel, [me, factor_rows, part, core, early, other],
        [jax.ShapeDtypeStruct((8 * LANES, LANES), jnp.float32)] * 2,
        [half, half, pltpu.VMEM((16 * LANES, LANES), jnp.float32)],
        6 * PAIRS * R2 * I1 * LATE)


def add_kernel(x_ref, o_ref):
    devices = x_ref.shape[0]
    total = jnp.sum(x_ref[...], axis=0) * (1.0 / (R2 * R3 * R4))
    o_ref[...] = jnp.broadcast_to(total[None], (devices,) + total.shape)


def add_parts(x):
    return pl.pallas_call(
        add_kernel, in_specs=[VMEM], out_specs=VMEM,
        out_shape=jax.ShapeDtypeStruct(x.shape, jnp.float32),
        compiler_params=pltpu.CompilerParams(vmem_limit_bytes=20 << 20),
        name="add",
    )(x)


def three(x):
    high = x.astype(jnp.bfloat16)
    rest = x - high.astype(jnp.float32)
    middle = rest.astype(jnp.bfloat16)
    return high, middle, (rest - middle.astype(jnp.float32)).astype(jnp.bfloat16)


def times(x, parts):
    n = x.shape[0]
    x1, x2, x3 = three(x)
    rows = ((1,), (0,))
    a = product(jnp.concatenate([x1, x2, x3], axis=0), parts[0][...], rows)
    b = product(jnp.concatenate([x1, x2], axis=0), parts[1][...], rows)
    c = product(x1, parts[2][...], rows)
    return a[:n] + ((a[n:2 * n] + b[:n]) + (a[2 * n:] + b[n:] + c))


def inner_rows(x):
    high, low = split(x)
    lanes = ((1,), (1,))
    return product(high, high, lanes) + (product(high, low, lanes) + product(low, high, lanes))


def inverse_factor(a):
    n = a.shape[0]
    blocks = n // 8
    rows = [a[8 * i:8 * i + 8, :] for i in range(blocks)]
    lane = lax.broadcasted_iota(jnp.int32, (8, n), 1)
    sub = lax.broadcasted_iota(jnp.int32, (8, n), 0)
    spread = lambda x: jnp.broadcast_to(x, (8, n))
    pivots = []
    for k in range(blocks):
        cols = [[spread(rows[i][:, 8 * k + j:8 * k + j + 1]) for j in range(8)]
                for i in range(k, blocks)]
        inside = (lane >= 8 * k) & (lane < 8 * k + 8)
        rows[k] = jnp.where(inside, jnp.where(lane - 8 * k == sub, 1.0, 0.0), rows[k])
        for i in range(k + 1, blocks):
            rows[i] = jnp.where(inside, 0.0, rows[i])
        pivot = jnp.zeros((8, n), jnp.float32)
        for j in range(0, 8, 2):
            p = spread(cols[0][j][j:j + 1, :])
            q = spread(cols[0][j][j + 1:j + 2, :])
            s = spread(cols[0][j + 1][j + 1:j + 2, :])
            det = p * s - q * q
            over_p, over_det = 1.0 / p, 1.0 / det
            row0, row1 = spread(rows[k][j:j + 1, :]), spread(rows[k][j + 1:j + 2, :])
            pivot = jnp.where(sub == j, p, jnp.where(sub == j + 1, det * over_p, pivot))
            u0, u1, u2 = s * over_det, q * over_det, p * over_det
            pair = {m: (spread(cols[0][m][j:j + 1, :]), spread(cols[0][m][j + 1:j + 2, :]))
                    for m in range(j + 2, 8)}
            for i in range(k, blocks):
                c0, c1 = cols[i - k][j], cols[i - k][j + 1]
                f0, f1 = c0 * u0 - c1 * u1, c1 * u2 - c0 * u1
                if i == k:
                    f0 = jnp.where(sub > j + 1, f0, jnp.where(sub == j + 1, q * over_p, 0.0))
                    f1 = jnp.where(sub > j + 1, f1, 0.0)
                rows[i] = rows[i] - (f0 * row0 + f1 * row1)
                for m in range(j + 2, 8):
                    cols[i - k][m] = cols[i - k][m] - (f0 * pair[m][0] + f1 * pair[m][1])
        pivots.append(pivot)
    return jnp.concatenate(
        [jnp.where(lane <= sub + 8 * k, rows[k] * lax.rsqrt(pivots[k]), 0.0)
         for k in range(blocks)], axis=0)


def sweep_kernel(core_ref, mine_ref, other_ref, start_ref, out_ref, packed_ref, gram_ref, image_ref, *parts):
    half = mine_ref.shape[0]
    me = core_ref[0]
    packed_ref[pl.ds(pl.multiple_of(me * half, half), half), :] = mine_ref[...]
    packed_ref[pl.ds(pl.multiple_of((1 - me) * half, half), half), :] = other_ref[...]
    row = lax.broadcasted_iota(jnp.int32, (LANES, LANES), 0)
    col = lax.broadcasted_iota(jnp.int32, (LANES, LANES), 1)
    span = lambda i: slice(i * LANES, (i + 1) * LANES)
    edge = packed_ref[span(len(EARLY_TILES)), :]
    for n, pair in enumerate(EARLY_TILES + (None,) + LATE_TILES):
        if pair is None:
            continue
        i, j = pair
        tile = packed_ref[span(n), :]
        if i == j:
            above = jnp.where(row < col, tile, 0.0)
            gram_ref[span(i), span(i)] = jnp.where(row <= col, tile, 0.0) + above.T
        else:
            gram_ref[span(i), span(j)] = tile
            gram_ref[span(j), span(i)] = tile.T
        if i == j and i in (2, 3):
            gram_ref[BODY:, i * LANES:i * LANES + 64] = tile[64:64 + TAIL, :64]
            gram_ref[BODY:, i * LANES + 64:(i + 1) * LANES] = tile[64 + TAIL:, :64]
    for k, i in enumerate((0, 1, 4)):
        gram_ref[span(i), BODY:] = edge[:, k * TAIL:(k + 1) * TAIL]
    gram_ref[BODY:, BODY:] = edge[:TAIL, 3 * TAIL:]
    gram_ref[BODY:, :LATE] = gram_ref[:LATE, BODY:].T
    gram_ref[BODY:, span(4)] = gram_ref[span(4), BODY:].T
    gram_ref[LATE:2 * LATE, BODY:] = gram_ref[BODY:, LATE:2 * LATE].T
    for part, value in zip(parts, three(gram_ref[...])):
        part[...] = value

    image_ref[...] = times(start_ref[...], parts)

    def sweep(_, carry):
        image = image_ref[...]
        ahead = times(image, parts)
        image_ref[...] = exact(inverse_factor(inner_rows(image)), ahead, ((1,), (0,)))
        return carry

    lax.fori_loop(0, ITERS - 1, sweep, 0)
    image = image_ref[...]
    inner = exact(image, image, ((1,), (1,)))
    out_ref[...] = exact(inverse_factor(inner), image, ((1,), (0,))) * math.sqrt(I1)


def sweeps(core, mine, other, start_rows):
    return pl.pallas_call(
        sweep_kernel,
        in_specs=[pl.BlockSpec(memory_space=pltpu.SMEM), VMEM, VMEM, VMEM], out_specs=VMEM,
        out_shape=jax.ShapeDtypeStruct((R1, I1), jnp.float32),
        scratch_shapes=[
            pltpu.VMEM((16 * LANES, LANES), jnp.float32), pltpu.VMEM((I1, I1), jnp.float32),
            pltpu.VMEM((R1, I1), jnp.float32)] + [pltpu.VMEM((I1, I1), jnp.bfloat16)] * 3,
        compiler_params=pltpu.CompilerParams(vmem_limit_bytes=32 << 20),
        name="sweeps",
    )(core, mine, other, start_rows)


def factors(mode2_factor, mode3_factor, mode4_factor, me):
    ranks = jnp.transpose(mode3_factor)
    turned = ranks[:NARROW_RANKS]
    turned = lax.dynamic_slice_in_dim(
        jnp.concatenate([turned, turned], axis=0), me * RANKS, NARROW_RANKS, 0)
    turned = jnp.concatenate([turned, ranks[NARROW_RANKS:]], axis=0)
    species = mode4_factor.shape[0]
    local = species // NARROW
    blocks = mode4_factor.reshape(NARROW, local, R4)[::-1].reshape(species, R4)
    blocks = lax.dynamic_slice_in_dim(
        jnp.concatenate([blocks, blocks], axis=0), (NARROW - 1 - me) * local, species, 0)
    weights = jnp.transpose(blocks)[:, None, :, None] * jnp.eye(8, dtype=jnp.float32)[None, :, None, :]
    weights = weights.reshape(R4 * 8, species * 8)
    cells = jnp.transpose(mode2_factor.reshape(WIDE, LOCAL2, R2), (2, 1, 0)).reshape(R2, I2)
    shares = lax.dynamic_slice_in_dim(
        jnp.concatenate([cells, cells], axis=0), me * SHARE, R2, 0)
    return turned, weights, cells, shares


def body(tensor, mode2_factor, mode3_factor, mode4_factor, start_basis):
    me = lax.axis_index("narrow")
    turned, weights, cells, shares = factors(mode2_factor, mode3_factor, mode4_factor, me)
    field = jnp.transpose(tensor, (0, 1, 3, 2))

    def send(blocks):
        got = list(blocks)
        for j in (1, 3, 2):
            ring = [(i, (i + j) % NARROW) for i in range(NARROW)]
            got[j] = lax.ppermute(blocks[j], "narrow", ring)
        return got

    def wide_exchange(x):
        return lax.all_to_all(x, WIDE_AXES, 0, 0, tiled=True).reshape(-1, LANES)

    blocks, rest = mode3(field, turned, CHUNKS[0])
    first = send(blocks)
    blocks, more = mode3(field, turned, CHUNKS[1])
    raw = wide_exchange(jnp.concatenate([rest, more], axis=1))
    first, blocks = lax.optimization_barrier((first, blocks))
    second = send(blocks)
    sums = species_sum(first, weights, SPECIES_COST)
    raw, sums = lax.optimization_barrier((raw, sums))
    part = wide_exchange(sums)
    shared = mode2_sum(raw, shares)
    second, shared = lax.optimization_barrier((second, shared))
    third = send(shared)
    last = wide_exchange(species_sum(second, weights, 10 ** 9))
    early, core = gram_first(part, cells)
    other = other_gram(third, weights)
    core_index = lax.axis_index("core").reshape(1)
    swap = [(0, 1), (1, 0)]
    keep, give = gram_last(core_index, last, core, early, other, cells)
    half = keep + lax.ppermute(give, "core", swap)
    chips = ("y", "z", "narrow")
    half = half.reshape(CHIPS, -1, LANES)
    half = add_parts(lax.all_to_all(half, chips, 0, 0, tiled=True))
    mine = lax.all_to_all(half, chips, 0, 0, tiled=True).reshape(-1, LANES)
    other = lax.ppermute(mine, "core", swap)
    return jnp.transpose(sweeps(core_index, mine, other, jnp.transpose(start_basis)))


def solution(mesh):
    fine = jax.sharding.Mesh(
        mesh.devices.reshape(4, 4, 2, NARROW), ("y", "z", "core", "narrow"))
    in_specs = (P("narrow", WIDE_AXES, None, None), P(), P(), P(), P())
    return jax.shard_map(body, mesh=fine, in_specs=in_specs, out_specs=P(), check_vma=False)
```

```python
import functools
import math

import jax
import jax.numpy as jnp
from jax import lax
from jax.experimental import pallas as pl
from jax.experimental.pallas import tpu as pltpu
from jax.sharding import PartitionSpec as P

I1 = 672
I2 = 128
I3 = 256
R1 = 96
R2 = 96
R3 = 96
R4 = 16
ITERS = 8
NARROW = 4
WIDE = 32
WIDE_AXES = ("y", "z", "core")
CHIPS = 64
LANES = 128
FULL = I1 // LANES
TAIL = I1 - FULL * LANES
BODY = FULL * LANES
LOCAL2 = I2 // WIDE
WIDE_RANKS = WIDE
NARROW_RANKS = R3 - WIDE_RANKS
RANKS = NARROW_RANKS // NARROW
PAIRS = RANKS * R4 // WIDE
SPECIES = 32
LOCAL4 = SPECIES // NARROW
SHARE = R2 // NARROW
CHUNKS = ((0, 1, 4), (2, 3))
EARLY = 3 * LANES + TAIL
LATE = 2 * LANES
EARLY_TILES = ((0, 0), (0, 1), (1, 1), (0, 4), (1, 4), (4, 4))
LATE_TILES = ((0, 2), (0, 3), (1, 2), (1, 3), (4, 2), (4, 3), (2, 2), (2, 3), (3, 3))
SPECIES_COST = 10 ** 11
VMEM = pl.BlockSpec(memory_space=pltpu.VMEM)


def whole(x):
    return pl.BlockSpec(x.shape, lambda i: (0,) * len(x.shape))


def split(x):
    high = x.astype(jnp.bfloat16)
    return high, (x - high.astype(jnp.float32)).astype(jnp.bfloat16)


def product(a, b, contract):
    return lax.dot_general(
        a, b, ((contract), ((), ())), preferred_element_type=jnp.float32
    )


def exact(a, b, contract):
    return lax.dot_general(
        a, b, ((contract), ((), ())),
        preferred_element_type=jnp.float32, precision=lax.Precision.HIGHEST,
    )


def left_product(weights, values):
    rows = weights.shape[0]
    w_high, w_low = split(weights)
    v_high, v_low = split(values)
    both = product(jnp.concatenate([w_high, w_low], axis=0), v_high, ((1,), (0,)))
    return both[:rows] + both[rows:] + product(w_high, v_low, ((1,), (0,)))


def mode3_kernel(joined, factor_ref, *refs):
    outs, rest_out, slabs = refs[-NARROW - 1:-1], refs[-1], refs[joined:-NARROW - 1]
    f_high, f_low = split(factor_ref[...])
    lanes = ((1,), (1,))
    some = outs[0].shape[0]
    stride = rest_out.shape[0] // WIDE
    start = 0
    if joined:
        earlier = refs[0]
        start = earlier.shape[0] // WIDE

        @pl.when(pl.program_id(0) == 0)
        def _():
            for r in range(WIDE):
                rest_out[r * stride:r * stride + start, :] = earlier[r * start:(r + 1) * start, :]

    for s in range(some):
        rows = jnp.concatenate([slab[s].reshape(-1, I3) for slab in slabs], axis=0)
        r_high, r_low = split(rows)
        both = product(jnp.concatenate([f_high, f_low], axis=0), r_high, lanes)
        done = both[:R3] + both[R3:] + product(f_high, r_low, lanes)
        for j, out in enumerate(outs):
            out[s] = done[j * RANKS:(j + 1) * RANKS]
        place = pl.program_id(0) * some + s
        for u in range(done.shape[1] // LANES):
            rest_out[pl.ds(start + u * LOCAL4 + place, WIDE, stride=stride), :] = done[
                NARROW_RANKS:, u * LANES:(u + 1) * LANES]


def mode3(field, factor_rows, chunk, earlier=None):
    species = field.shape[0]
    count = len(chunk)
    width = LOCAL2 * LANES * count
    some = 2
    in_specs = [pl.BlockSpec((R3, I3), lambda s: (0, 0))]
    args = [factor_rows]
    joined = 0
    if earlier is not None:
        joined = 1
        in_specs.append(pl.BlockSpec(earlier.shape, lambda s: (0, 0)))
        args.append(earlier)
    for tile in chunk:
        in_specs.append(pl.BlockSpec((some, LOCAL2, LANES, I3), lambda s, tile=tile: (s, 0, tile, 0)))
        args.append(field)
    if chunk == CHUNKS[0]:
        width += LANES
        in_specs.append(pl.BlockSpec((some, LOCAL2, TAIL, I3), lambda s: (s, 0, BODY // TAIL, 0)))
        args.append(field)
    shape = jax.ShapeDtypeStruct((species, RANKS, width), jnp.float32)
    rest = (WIDE * species * width // LANES + (earlier.shape[0] if joined else 0), LANES)
    out = pl.pallas_call(
        functools.partial(mode3_kernel, joined),
        grid=(species // some,),
        in_specs=in_specs,
        out_specs=[pl.BlockSpec((some, RANKS, width), lambda s: (s, 0, 0))] * NARROW
        + [pl.BlockSpec(rest, lambda s: (0, 0))],
        out_shape=[shape] * NARROW + [jax.ShapeDtypeStruct(rest, jnp.float32)],
        compiler_params=pltpu.CompilerParams(vmem_limit_bytes=58 << 20),
        cost_estimate=pl.CostEstimate(
            flops=6 * species * R3 * I3 * width,
            bytes_accessed=4 * species * width * (I3 + R3), transcendentals=0),
        name="mode3",
    )(*args)
    return out[:NARROW], out[NARROW]


def species_kernel(tiles, weights_ref, *refs):
    parts, out = refs[:NARROW], refs[NARROW]
    step = pl.program_id(0)
    rows = [p[...].reshape(-1, tiles * LANES) for p in parts]
    done = left_product(weights_ref[...], jnp.concatenate(rows, axis=0))
    for q in range(R4):
        for t in range(tiles):
            out[2 * q + step, t * PAIRS:(t + 1) * PAIRS, :] = done[
                q * 8:(q + 1) * 8, t * LANES:(t + 1) * LANES]


def species_sum(parts, weights, cost):
    species, ranks, width = parts[0].shape
    tiles = width // LANES
    rows = tiles * PAIRS
    return pl.pallas_call(
        functools.partial(species_kernel, tiles),
        grid=(ranks // 8,),
        in_specs=[pl.BlockSpec(weights.shape, lambda i: (0, 0))]
        + [pl.BlockSpec((species, 8, width), lambda i: (0, i, 0))] * NARROW,
        out_specs=pl.BlockSpec((WIDE, rows, LANES), lambda i: (0, 0, 0)),
        out_shape=jax.ShapeDtypeStruct((WIDE, rows, LANES), jnp.float32),
        compiler_params=pltpu.CompilerParams(vmem_limit_bytes=24 << 20),
        cost_estimate=pl.CostEstimate(
            flops=cost, bytes_accessed=4 * width * 24 * 48, transcendentals=0),
        name="species",
    )(weights, *parts)


def place_of(tile, b):
    if tile in CHUNKS[0]:
        return CHUNKS[0].index(tile) * LOCAL2 + b
    return len(CHUNKS[0]) * LOCAL2 + 1 + CHUNKS[1].index(tile) * LOCAL2 + b


def mode2_kernel(factor_ref, part_ref, *outs):
    f_high, f_low = split(factor_ref[...])
    doubled = jnp.concatenate([f_high, f_high], axis=1)
    stride = part_ref.shape[0] // WIDE
    tails = []
    for s in range(LOCAL4):
        def piece(place):
            return part_ref[pl.ds(place * LOCAL4 + s, WIDE, stride=stride), :]

        last = piece(len(CHUNKS[0]) * LOCAL2)
        cells = [
            jnp.concatenate([piece(place_of(t, b)) for t in range(FULL)]
                            + [last[:, b * TAIL:(b + 1) * TAIL]], axis=1)
            for b in range(LOCAL2)]
        v_high, v_low = split(jnp.concatenate(cells, axis=0))
        core = product(doubled, jnp.concatenate([v_high, v_low], axis=0), ((1,), (0,)))
        core = core + product(f_low, v_high, ((1,), (0,)))
        for j, out in enumerate(outs):
            rows = core[j * SHARE:(j + 1) * SHARE]
            for t in range(FULL):
                out[(s * FULL + t) * SHARE:(s * FULL + t + 1) * SHARE, :] = rows[:, t * LANES:(t + 1) * LANES]
        tails.append(core[:, BODY:])
        if s % 4 == 3:
            four = jnp.concatenate(tails[-4:], axis=1)
            start = (LOCAL4 * FULL + s // 4) * SHARE
            for j, out in enumerate(outs):
                out[start:start + SHARE, :] = four[j * SHARE:(j + 1) * SHARE]


def mode2_sum(part, factor_rows):
    rows = (LOCAL4 * FULL + LOCAL4 // 4) * SHARE
    shape = jax.ShapeDtypeStruct((rows, LANES), jnp.float32)
    args = [factor_rows, part]
    return pl.pallas_call(
        mode2_kernel, grid=(1,), in_specs=[whole(x) for x in args],
        out_specs=[whole(shape)] * NARROW, out_shape=[shape] * NARROW,
        compiler_params=pltpu.CompilerParams(vmem_limit_bytes=24 << 20),
        cost_estimate=pl.CostEstimate(
            flops=SPECIES_COST, bytes_accessed=6 << 20, transcendentals=0),
        name="mode2",
    )(*args)


def other_gram_kernel(weights_ref, *refs):
    parts, (out, high_ref, low_ref) = refs[:NARROW], refs[NARROW:]
    for block in range(SHARE // 8):
        rows = []
        for part in parts:
            for s in range(LOCAL4):
                def piece(n):
                    return part[n * SHARE + block * 8:n * SHARE + block * 8 + 8, :]

                tail = piece(LOCAL4 * FULL + s // 4)
                rows.append(jnp.concatenate(
                    [piece(s * FULL + t) for t in range(FULL)]
                    + [tail[:, s % 4 * TAIL:(s % 4 + 1) * TAIL]], axis=1))
        high, low = split(left_product(weights_ref[...], jnp.concatenate(rows, axis=0)))
        here = slice(block * R4 * 8, (block + 1) * R4 * 8)
        high_ref[here, :] = high
        low_ref[here, :] = low

    def inner(left, right):
        return inner_product(high_ref[:, left], low_ref[:, left], high_ref[:, right], low_ref[:, right])

    top = inner(slice(0, 256), slice(0, I1))
    middle = inner(slice(256, 512), slice(256, 512))
    below = inner(slice(512, I1), slice(256, I1))
    grid = {(i, j): tile_of(top, i, j) for i in range(2) for j in range(FULL)}
    grid.update({(2 + i, 2 + j): tile_of(middle, i, j) for i in range(2) for j in range(2)})
    grid.update({(4, 2 + j): tile_of(below, 0, j) for j in range(3)})
    for n, pair in enumerate(EARLY_TILES + (None,) + LATE_TILES):
        if pair is not None:
            out[n * LANES:(n + 1) * LANES, :] = grid[pair]
    put_edges(out, len(EARLY_TILES) * LANES, [top[:LANES, BODY:], top[LANES:, BODY:], below[:LANES, 256 + LANES:]],
              below[LANES:, 256 + LANES:])
    put_left(out, (len(EARLY_TILES) + 1) * LANES, below[LANES:, :256])


def other_gram(parts, weights):
    rows = SHARE * R4
    out = jax.ShapeDtypeStruct((16 * LANES, LANES), jnp.float32)
    args = [weights, *parts]
    half = pltpu.VMEM((rows, I1), jnp.bfloat16)
    return gram_call(other_gram_kernel, args, out, [half, half], 2 * SPECIES_COST)


def core_columns(factor, parts, store):
    f_high, f_low = split(factor)
    doubled = jnp.concatenate([f_high, f_high], axis=1)

    def piece(ref, place):
        return ref[pl.ds(place, WIDE, stride=ref.shape[0] // WIDE), :]

    for i in range(PAIRS):
        cells = []
        for b in range(LOCAL2):
            row = []
            for ref, count, tail in parts:
                row += [piece(ref, (t * LOCAL2 + b) * PAIRS + i) for t in range(count)]
                if tail:
                    last = piece(ref, LOCAL2 * count * PAIRS + i)
                    row.append(last[:, b * TAIL:(b + 1) * TAIL])
            cells.append(jnp.concatenate(row, axis=1))
        v_high, v_low = split(jnp.concatenate(cells, axis=0))
        core = product(doubled, jnp.concatenate([v_high, v_low], axis=0), ((1,), (0,)))
        store(i, *split(core + product(f_low, v_high, ((1,), (0,)))))


def inner_product(a_high, a_low, b_high, b_low):
    rows = ((0,), (0,))
    return product(a_high, b_high, rows) + product(a_high, b_low, rows) + product(a_low, b_high, rows)


def put_edges(out, place, edges, corner):
    edges = edges + [jnp.concatenate([corner] * (LANES // TAIL), axis=0)]
    out[place:place + LANES, :] = jnp.concatenate(edges, axis=1)


def put_left(out, place, left):
    for j, n in ((0, 6), (1, 8)):
        corner = place + n * LANES + 64
        out[corner:corner + TAIL, :64] = left[:, j * LANES:j * LANES + 64]
        out[corner + TAIL:corner + 2 * TAIL, :64] = left[:, j * LANES + 64:(j + 1) * LANES]


def tile_of(block, i, j):
    return block[i * LANES:(i + 1) * LANES, j * LANES:(j + 1) * LANES]


def gram_first_kernel(factor_ref, part_ref, out, core_ref):
    half = PAIRS * R2

    def store(i, high, low):
        core_ref[i * R2:(i + 1) * R2, :] = high
        core_ref[half + i * R2:half + (i + 1) * R2, :] = low

    core_columns(factor_ref[...], ((part_ref, 3, True),), store)
    two = slice(0, LATE)
    rest = slice(LATE, EARLY)
    top = inner_product(core_ref[:half, two], core_ref[half:, two], core_ref[:half, :], core_ref[half:, :])
    own = inner_product(core_ref[:half, rest], core_ref[half:, rest],
                        core_ref[:half, rest], core_ref[half:, rest])
    tiles = [tile_of(top, 0, 0), tile_of(top, 0, 1), tile_of(top, 1, 1),
             tile_of(top, 0, 2), tile_of(top, 1, 2), own[:LANES, :LANES]]
    for n, tile in enumerate(tiles):
        out[n * LANES:(n + 1) * LANES, :] = tile
    put_edges(out, len(tiles) * LANES,
              [top[:LANES, 3 * LANES:], top[LANES:, 3 * LANES:], own[:LANES, LANES:]], own[LANES:, LANES:])


def gram_last_kernel(me_ref, factor_ref, part_ref, core_ref, early_ref, other_ref, keep, give, high_ref, low_ref, out):
    half = PAIRS * R2

    def store(i, high, low):
        high_ref[i * R2:(i + 1) * R2, :] = high
        low_ref[i * R2:(i + 1) * R2, :] = low

    core_columns(factor_ref[...], ((part_ref, 2, False),), store)
    place = early_ref.shape[0]
    out[:place, :] = early_ref[...]
    high, low = high_ref[...], low_ref[...]
    above = inner_product(core_ref[:half, :], core_ref[half:, :], high, low)
    own = inner_product(high, low, high, low)
    tiles = [tile_of(above, i, j) for i in range(3) for j in range(2)]
    tiles += [tile_of(own, 0, 0), tile_of(own, 0, 1), tile_of(own, 1, 1)]
    for n, tile in enumerate(tiles):
        out[place + n * LANES:place + (n + 1) * LANES, :] = tile
    put_left(out, place, above[3 * LANES:, :])
    rows = keep.shape[0]
    me = me_ref[0]
    for ref, core in ((keep, me), (give, 1 - me)):
        here = pl.ds(pl.multiple_of(core * rows, rows), rows)
        ref[...] = out[here, :] + other_ref[here, :]


def gram_call(kernel, args, out_shape, scratch, flops):
    some = isinstance(out_shape, list)
    return pl.pallas_call(
        kernel, grid=(1,),
        in_specs=[pl.BlockSpec(memory_space=pltpu.SMEM) if x.ndim == 1 else whole(x) for x in args],
        out_specs=[whole(x) for x in out_shape] if some else whole(out_shape),
        out_shape=out_shape, scratch_shapes=scratch,
        compiler_params=pltpu.CompilerParams(vmem_limit_bytes=24 << 20),
        cost_estimate=pl.CostEstimate(flops=flops, bytes_accessed=8 << 20, transcendentals=0),
        name="gram",
    )(*args)


def gram_first(part, factor_rows):
    rows = PAIRS * R2
    return gram_call(
        gram_first_kernel, [factor_rows, part],
        [jax.ShapeDtypeStruct(((len(EARLY_TILES) + 1) * LANES, LANES), jnp.float32),
         jax.ShapeDtypeStruct((2 * rows, EARLY), jnp.bfloat16)],
        [], 4 * rows * EARLY * EARLY)


def gram_last(me, part, core, early, other, factor_rows):
    half = pltpu.VMEM((PAIRS * R2, LATE), jnp.bfloat16)
    return gram_call(
        gram_last_kernel, [me, factor_rows, part, core, early, other],
        [jax.ShapeDtypeStruct((8 * LANES, LANES), jnp.float32)] * 2,
        [half, half, pltpu.VMEM((16 * LANES, LANES), jnp.float32)],
        6 * PAIRS * R2 * I1 * LATE)


def add_kernel(x_ref, o_ref):
    devices = x_ref.shape[0]
    total = jnp.sum(x_ref[...], axis=0) * (1.0 / (R2 * R3 * R4))
    o_ref[...] = jnp.broadcast_to(total[None], (devices,) + total.shape)


def add_parts(x):
    return pl.pallas_call(
        add_kernel, in_specs=[VMEM], out_specs=VMEM,
        out_shape=jax.ShapeDtypeStruct(x.shape, jnp.float32),
        compiler_params=pltpu.CompilerParams(vmem_limit_bytes=20 << 20),
        name="add",
    )(x)


def three(x):
    high = x.astype(jnp.bfloat16)
    rest = x - high.astype(jnp.float32)
    middle = rest.astype(jnp.bfloat16)
    return high, middle, (rest - middle.astype(jnp.float32)).astype(jnp.bfloat16)


def times(x, parts):
    n = x.shape[0]
    x1, x2, x3 = three(x)
    rows = ((1,), (0,))
    a = product(jnp.concatenate([x1, x2, x3], axis=0), parts[0][...], rows)
    b = product(jnp.concatenate([x1, x2], axis=0), parts[1][...], rows)
    c = product(x1, parts[2][...], rows)
    return a[:n] + ((a[n:2 * n] + b[:n]) + (a[2 * n:] + b[n:] + c))


def inner_rows(x):
    high, low = split(x)
    lanes = ((1,), (1,))
    return product(high, high, lanes) + (product(high, low, lanes) + product(low, high, lanes))


def inverse_factor(a):
    n = a.shape[0]
    blocks = n // 8
    rows = [a[8 * i:8 * i + 8, :] for i in range(blocks)]
    lane = lax.broadcasted_iota(jnp.int32, (8, n), 1)
    sub = lax.broadcasted_iota(jnp.int32, (8, n), 0)
    spread = lambda x: jnp.broadcast_to(x, (8, n))
    columns = lambda i, k: [spread(rows[i][:, 8 * k + j:8 * k + j + 1]) for j in range(8)]
    pivots = []
    ahead = columns(0, 0)
    for k in range(blocks):
        cols = [ahead] + [columns(i, k) for i in range(k + 1, blocks)]
        ahead = columns(k + 1, k + 1) if k + 1 < blocks else []
        inside = (lane >= 8 * k) & (lane < 8 * k + 8)
        rows[k] = jnp.where(inside, jnp.where(lane - 8 * k == sub, 1.0, 0.0), rows[k])
        for i in range(k + 1, blocks):
            rows[i] = jnp.where(inside, 0.0, rows[i])
        pivot = jnp.zeros((8, n), jnp.float32)
        for j in range(0, 8, 2):
            p = spread(cols[0][j][j:j + 1, :])
            q = spread(cols[0][j][j + 1:j + 2, :])
            s = spread(cols[0][j + 1][j + 1:j + 2, :])
            det = p * s - q * q
            over_p, over_det = 1.0 / p, 1.0 / det
            row0, row1 = spread(rows[k][j:j + 1, :]), spread(rows[k][j + 1:j + 2, :])
            pivot = jnp.where(sub == j, p, jnp.where(sub == j + 1, det * over_p, pivot))
            u0, u1, u2 = s * over_det, q * over_det, p * over_det
            pair = {m: (spread(cols[0][m][j:j + 1, :]), spread(cols[0][m][j + 1:j + 2, :]))
                    for m in range(j + 2, 8)}
            cross = [(spread(cols[1][j][m:m + 1, :]), spread(cols[1][j + 1][m:m + 1, :]))
                     for m in range(len(ahead))]
            for i in range(k, blocks):
                c0, c1 = cols[i - k][j], cols[i - k][j + 1]
                f0, f1 = c0 * u0 - c1 * u1, c1 * u2 - c0 * u1
                if i == k:
                    f0 = jnp.where(sub > j + 1, f0, jnp.where(sub == j + 1, q * over_p, 0.0))
                    f1 = jnp.where(sub > j + 1, f1, 0.0)
                if i == k + 1:
                    ahead = [x - (f0 * c[0] + f1 * c[1]) for x, c in zip(ahead, cross)]
                rows[i] = rows[i] - (f0 * row0 + f1 * row1)
                for m in range(j + 2, 8):
                    cols[i - k][m] = cols[i - k][m] - (f0 * pair[m][0] + f1 * pair[m][1])
        pivots.append(pivot)
    return jnp.concatenate(
        [jnp.where(lane <= sub + 8 * k, rows[k] * lax.rsqrt(pivots[k]), 0.0)
         for k in range(blocks)], axis=0)


def sweep_kernel(core_ref, mine_ref, other_ref, start_ref, out_ref, packed_ref, gram_ref, image_ref, *parts):
    half = mine_ref.shape[0]
    me = core_ref[0]
    packed_ref[pl.ds(pl.multiple_of(me * half, half), half), :] = mine_ref[...]
    packed_ref[pl.ds(pl.multiple_of((1 - me) * half, half), half), :] = other_ref[...]
    row = lax.broadcasted_iota(jnp.int32, (LANES, LANES), 0)
    col = lax.broadcasted_iota(jnp.int32, (LANES, LANES), 1)
    span = lambda i: slice(i * LANES, (i + 1) * LANES)
    edge = packed_ref[span(len(EARLY_TILES)), :]
    for n, pair in enumerate(EARLY_TILES + (None,) + LATE_TILES):
        if pair is None:
            continue
        i, j = pair
        tile = packed_ref[span(n), :]
        if i == j:
            above = jnp.where(row < col, tile, 0.0)
            gram_ref[span(i), span(i)] = jnp.where(row <= col, tile, 0.0) + above.T
        else:
            gram_ref[span(i), span(j)] = tile
            gram_ref[span(j), span(i)] = tile.T
        if i == j and i in (2, 3):
            gram_ref[BODY:, i * LANES:i * LANES + 64] = tile[64:64 + TAIL, :64]
            gram_ref[BODY:, i * LANES + 64:(i + 1) * LANES] = tile[64 + TAIL:, :64]
    for k, i in enumerate((0, 1, 4)):
        gram_ref[span(i), BODY:] = edge[:, k * TAIL:(k + 1) * TAIL]
    gram_ref[BODY:, BODY:] = edge[:TAIL, 3 * TAIL:]
    gram_ref[BODY:, :LATE] = gram_ref[:LATE, BODY:].T
    gram_ref[BODY:, span(4)] = gram_ref[span(4), BODY:].T
    gram_ref[LATE:2 * LATE, BODY:] = gram_ref[BODY:, LATE:2 * LATE].T
    for part, value in zip(parts, three(gram_ref[...])):
        part[...] = value

    image_ref[...] = times(start_ref[...], parts)

    def sweep(_, carry):
        image = image_ref[...]
        ahead = times(image, parts)
        image_ref[...] = exact(inverse_factor(inner_rows(image)), ahead, ((1,), (0,)))
        return carry

    lax.fori_loop(0, ITERS - 1, sweep, 0)
    image = image_ref[...]
    inner = exact(image, image, ((1,), (1,)))
    out_ref[...] = exact(inverse_factor(inner), image, ((1,), (0,))) * math.sqrt(I1)


def sweeps(core, mine, other, start_rows):
    return pl.pallas_call(
        sweep_kernel,
        in_specs=[pl.BlockSpec(memory_space=pltpu.SMEM), VMEM, VMEM, VMEM], out_specs=VMEM,
        out_shape=jax.ShapeDtypeStruct((R1, I1), jnp.float32),
        scratch_shapes=[
            pltpu.VMEM((16 * LANES, LANES), jnp.float32), pltpu.VMEM((I1, I1), jnp.float32),
            pltpu.VMEM((R1, I1), jnp.float32)] + [pltpu.VMEM((I1, I1), jnp.bfloat16)] * 3,
        compiler_params=pltpu.CompilerParams(vmem_limit_bytes=32 << 20),
        name="sweeps",
    )(core, mine, other, start_rows)


def factors(mode2_factor, mode3_factor, mode4_factor, me):
    ranks = jnp.transpose(mode3_factor)
    turned = ranks[:NARROW_RANKS]
    turned = lax.dynamic_slice_in_dim(
        jnp.concatenate([turned, turned], axis=0), me * RANKS, NARROW_RANKS, 0)
    turned = jnp.concatenate([turned, ranks[NARROW_RANKS:]], axis=0)
    species = mode4_factor.shape[0]
    local = species // NARROW
    blocks = mode4_factor.reshape(NARROW, local, R4)[::-1].reshape(species, R4)
    blocks = lax.dynamic_slice_in_dim(
        jnp.concatenate([blocks, blocks], axis=0), (NARROW - 1 - me) * local, species, 0)
    weights = jnp.transpose(blocks)[:, None, :, None] * jnp.eye(8, dtype=jnp.float32)[None, :, None, :]
    weights = weights.reshape(R4 * 8, species * 8)
    cells = jnp.transpose(mode2_factor.reshape(WIDE, LOCAL2, R2), (2, 1, 0)).reshape(R2, I2)
    shares = lax.dynamic_slice_in_dim(
        jnp.concatenate([cells, cells], axis=0), me * SHARE, R2, 0)
    return turned, weights, cells, shares


def body(tensor, mode2_factor, mode3_factor, mode4_factor, start_basis):
    me = lax.axis_index("narrow")
    turned, weights, cells, shares = factors(mode2_factor, mode3_factor, mode4_factor, me)
    field = jnp.transpose(tensor, (0, 1, 3, 2))

    def send(blocks):
        got = list(blocks)
        for j in (1, 3, 2):
            ring = [(i, (i + j) % NARROW) for i in range(NARROW)]
            got[j] = lax.ppermute(blocks[j], "narrow", ring)
        return got

    def wide_exchange(x):
        return lax.all_to_all(x, WIDE_AXES, 0, 0, tiled=True).reshape(-1, LANES)

    blocks, rest = mode3(field, turned, CHUNKS[0])
    first = send(blocks)
    blocks, rest = mode3(field, turned, CHUNKS[1], rest)
    raw = wide_exchange(rest.reshape(WIDE, -1, LANES))
    first, blocks = lax.optimization_barrier((first, blocks))
    second = send(blocks)
    sums = species_sum(first, weights, SPECIES_COST)
    raw, sums = lax.optimization_barrier((raw, sums))
    part = wide_exchange(sums)
    shared = mode2_sum(raw, shares)
    second, shared = lax.optimization_barrier((second, shared))
    third = send(shared)
    last = wide_exchange(species_sum(second, weights, 10 ** 9))
    early, core = gram_first(part, cells)
    other = other_gram(third, weights)
    core_index = lax.axis_index("core").reshape(1)
    swap = [(0, 1), (1, 0)]
    keep, give = gram_last(core_index, last, core, early, other, cells)
    half = keep + lax.ppermute(give, "core", swap)
    chips = ("y", "z", "narrow")
    half = half.reshape(CHIPS, -1, LANES)
    half = add_parts(lax.all_to_all(half, chips, 0, 0, tiled=True))
    mine = lax.all_to_all(half, chips, 0, 0, tiled=True).reshape(-1, LANES)
    other = lax.ppermute(mine, "core", swap)
    return jnp.transpose(sweeps(core_index, mine, other, jnp.transpose(start_basis)))


def solution(mesh):
    fine = jax.sharding.Mesh(
        mesh.devices.reshape(4, 4, 2, NARROW), ("y", "z", "core", "narrow"))
    in_specs = (P("narrow", WIDE_AXES, None, None), P(), P(), P(), P())
    return jax.shard_map(body, mesh=fine, in_specs=in_specs, out_specs=P(), check_vma=False)
```
